128 devices in a mesh: seqin: 4 (over y), seqout: 8 (over x, core), head: 4 (over z).
Axes of the slice: x: 4, y: 4, z: 4, core: 2. Of those that a mesh axis runs over, the one named last changes fastest.
Arguments:
- queries: bfloat16 [32768, 4096], P(('seqin', 'seqout'), 'head'), may hold values from -6 to 6
- keys: bfloat16 [32768, 4096], P(('seqin', 'seqout'), 'head'), may hold values from -6 to 6
- values: bfloat16 [32768, 4096], P(('seqin', 'seqout'), 'head'), may hold values from -120 to 120
- gain: float32 [4096], P('head'), may hold values from 0.5 to 1.5
- cotangent: bfloat16 [32768, 4096], P(('seqin', 'seqout'), 'head'), may hold values from -6 to 6
Outputs:
- mixed: bfloat16 [32768, 4096], P(('seqin', 'seqout'), 'head')
- grad_queries: bfloat16 [32768, 4096], P(('seqin', 'seqout'), 'head')
- grad_keys: bfloat16 [32768, 4096], P(('seqin', 'seqout'), 'head')
- grad_values: bfloat16 [32768, 4096], P(('seqin', 'seqout'), 'head')
The draws below stay inside these ranges and needn't reach their ends.
All inputs are finite; a program needn't handle non-finite values.
Results may differ from the reference program's by a relative error of at most 0.0089.
Values sent between devices are 32-bit elements; how exact they have to be, the bound alone decides.
No kernel may reach another device: no remote copies, remote signals or barrier semaphores. Data moves between devices by JAX's collectives and lax.ppermute only.
A program may use at most 192 MiB of HBM per device.

```python
import math
import jax
import jax.numpy as jnp
from jax import lax

H = 32
E = 128
D = 4096
BLOCK = 512
TOKENS = 32768


def draw_values(key, part):
    key = jax.random.fold_in(key, 7)
    first, second, third = jax.random.split(key, 3)
    base = jnp.clip(jax.random.normal(first, (TOKENS, D), jnp.float32), -4.0, 4.0)
    rise = math.log(3.0)
    rows = jnp.exp(jax.random.uniform(second, (TOKENS, 1), jnp.float32) * math.log(10.0))
    ramp = jnp.arange(D, dtype=jnp.float32)[None, :] / (D - 1)
    cols = jnp.exp(rise * ramp) * jnp.exp(jax.random.uniform(third, (1, D), jnp.float32) * math.log(4.0))
    return (base * rows * cols / 6.0).astype(jnp.bfloat16)


def levels(own_key, dims, pieces, smallest, high):
    level, own = 1.0, jax.random.fold_in(own_key, 6)
    for axis_at, shards_of in pieces:
        heights = jnp.exp(jax.random.uniform(jax.random.fold_in(own, axis_at), (shards_of,), jnp.float32, smallest / len(pieces), high / len(pieces)))
        level = level * jnp.repeat(heights, dims[axis_at] // shards_of).reshape([-1 if axis == axis_at else 1 for axis in range(len(dims))])
    return level


def noise(stream_key, shape, scale, limit, cuts=(), held_as=jnp.bfloat16):
    drawn = scale * jax.random.normal(stream_key, shape, jnp.float32)
    if cuts:
        drawn = drawn * levels(stream_key, shape, cuts, -0.22, 0.18)
    return jnp.clip(drawn, -limit, limit).astype(held_as)


def setup_inputs(seed: int = 0) -> dict:
    streams_of = jax.random.split(jax.random.key(seed), 6)
    return {
        "queries": noise(streams_of[0], (TOKENS, D), 1.0, 6.0, ((0, 32), (1, 4))),
        "keys": noise(streams_of[1], (TOKENS, D), 1.0, 6.0, ((0, 32), (1, 4))),
        "values": draw_values(jax.random.fold_in(streams_of[5], 71), 0),
        "gain": jnp.clip(1.0 + 0.1 * jax.random.normal(streams_of[3], (D,), jnp.float32), 0.5, 1.5),
        "cotangent": noise(streams_of[4], (TOKENS, D), 1.0, 6.0, ((0, 32), (1, 4))),
    }


HIGH = lax.Precision.HIGHEST

def features(x):
    xf = x.astype(jnp.float32)
    return jnp.where(xf > 0, xf + 1.0, jnp.exp(jnp.minimum(xf, 0.0))).astype(jnp.bfloat16)

def slope(x):
    xf = x.astype(jnp.float32)
    return jnp.where(xf > 0, 1.0, jnp.exp(jnp.minimum(xf, 0.0)))

def reference(queries, keys, values, gain, cotangent):
    nblk = TOKENS // BLOCK
    shape4 = (nblk, BLOCK, H, E)
    fq = features(queries).reshape(shape4)
    fk = features(keys).reshape(shape4)
    vv = values.reshape(shape4)
    causal = jnp.arange(BLOCK)[:, None] >= jnp.arange(BLOCK)[None, :]

    def forward(carry, blk):
        state, norm = carry
        bq, bk, bv = blk
        bq32 = bq.astype(jnp.float32)
        bk32 = bk.astype(jnp.float32)
        bv32 = bv.astype(jnp.float32)
        scores = jnp.einsum('thd,shd->hts', bq32, bk32)
        wts = jnp.where(causal[None], scores, 0.0).astype(jnp.bfloat16).astype(jnp.float32)
        numer = jnp.einsum('hts,she->the', wts, bv32) + jnp.einsum('thd,hde->the', bq32, state, precision=HIGH)
        denom = jnp.einsum('hts->th', wts) + jnp.einsum('thd,hd->th', bq32, norm, precision=HIGH)
        attn = numer / denom[:, :, None]
        new_state = state + jnp.einsum('shd,she->hde', bk32, bv32)
        new_norm = norm + lax.optimization_barrier(jnp.sum(bk32, axis=0))
        return ((new_state, new_norm), (attn, denom, state, norm))
    init = (jnp.zeros((H, E, E), jnp.float32), jnp.zeros((H, E), jnp.float32))
    _, (attn, denom, states, norms) = lax.scan(forward, init, (fq, fk, vv))
    flat = attn.reshape(TOKENS, D)
    scale = lax.rsqrt(lax.optimization_barrier(jnp.sum(flat * flat, axis=1)) / D + 1e-06)
    mixed = (flat * scale[:, None] * gain[None, :]).astype(jnp.bfloat16)
    weighted = cotangent.astype(jnp.float32) * gain[None, :]
    proj = lax.optimization_barrier(jnp.sum(weighted * flat, axis=1))
    d_attn = scale[:, None] * weighted - flat * (scale ** 3 * proj / D)[:, None]
    d4 = d_attn.reshape(nblk, BLOCK, H, E)
    g_num = (d4 / denom[..., None]).astype(jnp.bfloat16)
    g_den = -lax.optimization_barrier(jnp.sum(d4 * attn, axis=3)) / denom

    def backward(carry, blk):
        later, later_den = carry
        bq, bk, bv, gn, gd, state, norm = blk
        bq32 = bq.astype(jnp.float32)
        bk32 = bk.astype(jnp.float32)
        bv32 = bv.astype(jnp.float32)
        gn32 = gn.astype(jnp.float32)
        scores = jnp.einsum('thd,shd->hts', bq32, bk32)
        wts = jnp.where(causal[None], scores, 0.0).astype(jnp.bfloat16).astype(jnp.float32)
        mix = jnp.einsum('the,she->hts', gn32, bv32) + gd.T[:, :, None]
        mixw = jnp.where(causal[None], mix, 0.0).astype(jnp.bfloat16).astype(jnp.float32)
        dfq = jnp.einsum('hts,shd->thd', mixw, bk32) + jnp.einsum('the,hde->thd', gn32, state, precision=HIGH) + gd[:, :, None] * norm[None]
        dfk = jnp.einsum('hts,thd->shd', mixw, bq32) + jnp.einsum('hde,she->shd', later, bv32, precision=HIGH) + later_den[None]
        dvv = jnp.einsum('hts,the->she', wts, gn32) + jnp.einsum('shd,hde->she', bk32, later, precision=HIGH)
        new_later = later + jnp.einsum('thd,the->hde', bq32, gn32)
        new_den = later_den + jnp.einsum('th,thd->hd', gd, bq32, precision=HIGH)
        return ((new_later, new_den), (dfq, dfk, dvv))
    _, (dfq, dfk, dvv) = lax.scan(backward, init, (fq, fk, vv, g_num, g_den, states, norms), reverse=True)
    grad_queries = (dfq.reshape(TOKENS, D) * slope(queries)).astype(jnp.bfloat16)
    grad_keys = (dfk.reshape(TOKENS, D) * slope(keys)).astype(jnp.bfloat16)
    grad_values = dvv.reshape(TOKENS, D).astype(jnp.bfloat16)
    return (mixed, grad_queries, grad_keys, grad_values)
```

```python
import functools

import jax
import jax.numpy as jnp
from jax import lax
from jax.experimental import pallas as pl
from jax.experimental.pallas import tpu as pltpu
from jax.sharding import PartitionSpec as P

E = 128
D = 4096
ROWS = 1024
BLOCK = 512
HALF = 256
AUG = E + 8
F32 = jnp.float32
BF16 = jnp.bfloat16
VMEM_LIMIT = 24 * 1024 * 1024


def phi(x):
    xf = x.astype(F32)
    return jnp.where(xf > 0, xf + 1.0, jnp.exp(jnp.minimum(xf, 0.0))).astype(BF16)


def slope(x):
    xf = x.astype(F32)
    return jnp.where(xf > 0, 1.0, jnp.exp(jnp.minimum(xf, 0.0)))


def split(x):
    hi = x.astype(BF16)
    return hi, (x - hi.astype(F32)).astype(BF16)


def dot(a, b, ca=1, cb=0):
    return lax.dot_general(a, b, (((ca,), (cb,)), ((), ())), preferred_element_type=F32)


def iota(shape, dim):
    return lax.broadcasted_iota(jnp.int32, shape, dim)


def column(row):
    return jnp.transpose(jnp.broadcast_to(row, (E, E)))


def sums_kernel(c_ref, k_ref, v_ref, total_ref, first_ref):
    parts = []
    for b in range(2):
        rows = pl.ds(b * BLOCK, BLOCK)
        fk = phi(k_ref[rows, :])
        kv = dot(fk, v_ref[rows, :], 0, 0)
        z = jnp.sum(fk.astype(F32), axis=0, keepdims=True)
        parts.append((kv, jnp.broadcast_to(z, (8, E))))
    first_ref[0, :E, :] = parts[0][0]
    first_ref[0, E:, :] = parts[0][1]
    total_ref[0, :E, :] = parts[0][0] + parts[1][0]
    total_ref[0, E:, :] = parts[0][1] + parts[1][1]


def intra_kernel(c_ref, q_ref, k_ref, v_ref, *rest):
    nd_ref = rest[-1]
    tri = iota((HALF, HALF), 0) >= iota((HALF, HALF), 1)
    for b in range(2):
        rows = pl.ds(b * BLOCK, BLOCK)
        fq, fk = phi(q_ref[rows, :]), phi(k_ref[rows, :])
        va = jnp.concatenate([v_ref[rows, :], jnp.ones((BLOCK, E), BF16)], axis=1)
        w00 = jnp.where(tri, dot(fq[:HALF], fk[:HALF], 1, 1), 0.0).astype(BF16)
        w10 = dot(fq[HALF:], fk[:HALF], 1, 1).astype(BF16)
        w11 = jnp.where(tri, dot(fq[HALF:], fk[HALF:], 1, 1), 0.0).astype(BF16)
        nd_ref[0, pl.ds(b * BLOCK, HALF), :] = dot(w00, va[:HALF])
        nd_ref[0, pl.ds(b * BLOCK + HALF, HALF), :] = dot(jnp.concatenate([w10, w11], axis=1), va)


def attn_kernel(c_ref, q_ref, ct_ref, gain_ref, nd_ref, st_ref, first_ref, attn_ref, inv_ref, sums_ref, sq_acc, pr_acc):
    j = pl.program_id(0)

    @pl.when(j == 0)
    def _():
        sq_acc[...] = jnp.zeros_like(sq_acc)
        pr_acc[...] = jnp.zeros_like(pr_acc)

    for b in range(2):
        rows = pl.ds(b * BLOCK, BLOCK)
        aug = st_ref[0] + first_ref[0] if b else st_ref[0]
        s_hi, s_lo = split(aug[:E])
        n_hi, n_lo = split(column(aug[E : E + 1]))
        rhs = jnp.concatenate([jnp.concatenate([s_hi, n_hi], axis=1), jnp.concatenate([s_lo, n_lo], axis=1)], axis=0)
        fq = phi(q_ref[rows, :])
        nd = nd_ref[0, rows, :] + dot(jnp.concatenate([fq, fq], axis=1), rhs)
        inv = 1.0 / nd[:, E:]
        attn = nd[:, :E] * inv
        attn_ref[0, rows, :] = attn
        inv_ref[0, rows, :] = inv
        sq_acc[rows, :] += attn * attn
        pr_acc[rows, :] += ct_ref[rows, :].astype(F32) * gain_ref[...] * attn

    @pl.when(j == pl.num_programs(0) - 1)
    def _():
        for i in range(8):
            rows = pl.ds(i * E, E)
            sums_ref[pl.ds(i, 1), :] = jnp.sum(jnp.transpose(sq_acc[rows, :]), axis=0, keepdims=True)
            sums_ref[pl.ds(8 + i, 1), :] = jnp.sum(jnp.transpose(pr_acc[rows, :]), axis=0, keepdims=True)


def spread(sc_ref, scale_ref, coef_ref):
    for i in range(8):
        rows = pl.ds(i * E, E)
        scale_ref[rows, :] = column(sc_ref[pl.ds(i, 1), :])
        if coef_ref is not None:
            coef_ref[rows, :] = column(sc_ref[pl.ds(8 + i, 1), :])


def grad_kernel(c_ref, q_ref, ct_ref, gain_ref, sc_ref, attn_ref, inv_ref, g_ref, total_ref, last_ref, scale_ref, coef_ref):
    @pl.when(pl.program_id(0) == 0)
    def _():
        spread(sc_ref, scale_ref, coef_ref)

    parts = []
    lane = iota((BLOCK, E), 1)
    ones = jnp.ones((2 * E, E), BF16)
    for b in range(2):
        rows = pl.ds(b * BLOCK, BLOCK)
        attn, inv = attn_ref[0, rows, :], inv_ref[0, rows, :]
        weighted = ct_ref[rows, :].astype(F32) * gain_ref[...]
        d_attn = scale_ref[rows, :] * weighted - attn * coef_ref[rows, :]
        g = (d_attn * inv).astype(BF16)
        p_hi, p_lo = split(d_attn * attn)
        gd = -dot(jnp.concatenate([p_hi, p_lo], axis=1), ones) * inv
        gd_hi, gd_lo = split(gd)
        aug = jnp.where((lane == 0) | (lane == 2), gd_hi, jnp.where(lane == 1, gd_lo, jnp.zeros_like(gd_lo)))
        g_ref[0, rows, :] = jnp.concatenate([g, aug], axis=1)
        fq = phi(q_ref[rows, :])
        rev = dot(fq, g, 0, 0)
        rden = jnp.sum(gd * fq.astype(F32), axis=0, keepdims=True)
        parts.append((rev, jnp.broadcast_to(rden, (8, E))))
    last_ref[0, :E, :] = parts[1][0]
    last_ref[0, E:, :] = parts[1][1]
    total_ref[0, :E, :] = parts[0][0] + parts[1][0]
    total_ref[0, E:, :] = parts[0][1] + parts[1][1]


def back_kernel(c_ref, q_ref, k_ref, v_ref, gain_ref, sc_ref, attn_ref, g_ref, st_ref, first_ref, *rest):
    dq_ref, mixed_ref, dk_ref, dv_ref, scale_ref = rest[-5:]

    @pl.when(pl.program_id(0) == 0)
    def _():
        spread(sc_ref, scale_ref, None)

    low = iota((HALF, HALF), 0) >= iota((HALF, HALF), 1)
    up = iota((HALF, HALF), 0) <= iota((HALF, HALF), 1)
    flag = (iota((BLOCK, E), 1) < 2).astype(BF16)
    lane = iota((E, E), 1)
    for b in range(2):
        rows = pl.ds(b * BLOCK, BLOCK)
        q, k, v = q_ref[rows, :], k_ref[rows, :], v_ref[rows, :]
        fq, fk = phi(q), phi(k)
        ga = g_ref[0, rows, :]
        g = ga[:, :E]
        va = jnp.concatenate([v, flag], axis=1)
        m00 = jnp.where(low, dot(ga[:HALF], va[:HALF], 1, 1), 0.0).astype(BF16)
        m10 = dot(ga[HALF:], va[:HALF], 1, 1).astype(BF16)
        m11 = jnp.where(low, dot(ga[HALF:], va[HALF:], 1, 1), 0.0).astype(BF16)
        w00 = jnp.where(up, dot(fk[:HALF], fq[:HALF], 1, 1), 0.0).astype(BF16)
        w10 = dot(fk[:HALF], fq[HALF:], 1, 1).astype(BF16)
        w11 = jnp.where(up, dot(fk[HALF:], fq[HALF:], 1, 1), 0.0).astype(BF16)
        aug = st_ref[0] + first_ref[0] if b else st_ref[0]
        s_hi, s_lo = split(aug[:E])
        n_hi, n_lo = split(column(aug[E : E + 1]))
        naug = jnp.where(lane < 2, n_hi, jnp.where(lane == 2, n_lo, jnp.zeros_like(n_lo)))
        rhs = jnp.concatenate([s_hi, s_lo, naug], axis=1)
        dfq = dot(jnp.concatenate([g, ga], axis=1), rhs, 1, 1)
        dfq = dfq + jnp.concatenate([dot(m00, fk[:HALF]), dot(jnp.concatenate([m10, m11], axis=1), fk)], axis=0)
        dq_ref[rows, :] = (dfq * slope(q)).astype(BF16)
        mixed_ref[rows, :] = (attn_ref[0, rows, :] * scale_ref[rows, :] * gain_ref[...]).astype(BF16)
        dk_ref[0, pl.ds(b * BLOCK, HALF), :] = dot(jnp.concatenate([m00, m10], axis=0), fq, 0, 0)
        dk_ref[0, pl.ds(b * BLOCK + HALF, HALF), :] = dot(m11, fq[HALF:], 0, 0)
        dv_ref[0, pl.ds(b * BLOCK, HALF), :] = dot(jnp.concatenate([w00, w10], axis=1), g)
        dv_ref[0, pl.ds(b * BLOCK + HALF, HALF), :] = dot(w11, g[HALF:])


def last_kernel(c_ref, k_ref, v_ref, dk_ref, dv_ref, lt_ref, last_ref, *rest):
    gk_ref, gv_ref = rest[-2:]
    for b in range(2):
        rows = pl.ds(b * BLOCK, BLOCK)
        k, v = k_ref[rows, :], v_ref[rows, :]
        fk = phi(k)
        aug = lt_ref[0] if b else lt_ref[0] + last_ref[0]
        l_hi, l_lo = split(aug[:E])
        dfk = dk_ref[0, rows, :] + dot(jnp.concatenate([v, v], axis=1), jnp.concatenate([l_hi, l_lo], axis=1), 1, 1)
        dfk = dfk + aug[E : E + 1]
        dv = dv_ref[0, rows, :] + dot(jnp.concatenate([fk, fk], axis=1), jnp.concatenate([l_hi, l_lo], axis=0))
        gk_ref[rows, :] = (dfk * slope(k)).astype(BF16)
        gv_ref[rows, :] = dv.astype(BF16)


def call(kernel, c, start, count, ins, outs, scratch=(), cost=(0, 0)):
    def head(j, c):
        return lax.rem(4 * c[0] + start + j, 8)

    def spec(kind, shape):
        if kind == "cols":
            return pl.BlockSpec((ROWS, E), lambda j, c: (0, head(j, c)))
        if kind == "gain":
            return pl.BlockSpec((1, E), lambda j, c: (0, head(j, c)))
        if kind == "whole":
            return pl.BlockSpec(shape, lambda j, c: (0,) * len(shape))
        if kind == "step":
            return pl.BlockSpec((1,) + shape[1:], lambda j, c: (j,) + (0,) * (len(shape) - 1))
        return pl.BlockSpec((1,) + shape[1:], lambda j, c: (start + j,) + (0,) * (len(shape) - 1))

    arrays = [a for a, _ in ins]
    specs = [spec(kind, a.shape) for a, kind in ins]
    aliases = {}
    for i, (_, _, _, into) in enumerate(outs):
        if into is not None:
            aliases[1 + len(arrays)] = i
            arrays.append(into)
            specs.append(pl.BlockSpec(memory_space=pl.ANY))
    return pl.pallas_call(
        kernel,
        out_shape=[jax.ShapeDtypeStruct(s, t) for s, t, _, _ in outs],
        grid_spec=pltpu.PrefetchScalarGridSpec(
            num_scalar_prefetch=1,
            grid=(count,),
            in_specs=specs,
            out_specs=[spec(kind, s) for s, _, kind, _ in outs],
            scratch_shapes=list(scratch),
        ),
        input_output_aliases=aliases,
        compiler_params=pltpu.CompilerParams(vmem_limit_bytes=VMEM_LIMIT),
        cost_estimate=pl.CostEstimate(flops=count * cost[0], bytes_accessed=count * cost[1], transcendentals=0),
    )(c, *arrays)


CORE = [(i, i ^ 1) for i in range(8)]


def swap(x):
    return lax.ppermute(x, "seqout", CORE)


def pick(parts, at):
    return lax.dynamic_index_in_dim(parts, at, 0, keepdims=False)


def scan(keep, other, x, reverse):
    total = keep + other
    own = pick(total, x)
    got = [own]
    for k in (1, 2, 3):
        got.append(lax.ppermute(pick(total, (x + k) % 4), "seqout", [(i, (i + 2 * k) % 8) for i in range(8)]))
    row = got[0] + got[1] + got[2] + got[3]

    def before(at):
        parts = []
        for m in range(4):
            source = (x - m) % 4
            reached = source > at if reverse else source < at
            parts.append(jnp.where(reached, got[m], 0.0))
        return parts[0] + parts[1] + parts[2] + parts[3]

    rows = []
    for k in (1, 2, 3):
        pairs = [(i, i - k) if reverse else (i, i + k) for i in range(4)]
        rows.append(lax.ppermute(row, "seqin", [(a, b) for a, b in pairs if 0 <= b < 4]))
    base = rows[0] + rows[1] + rows[2]
    heads = jnp.arange(4)[:, None, None]
    out = jnp.where(heads == x, (base + before(x))[None], 0.0)
    for k in (1, 2, 3):
        sent = base + before((x + k) % 4)
        came = lax.ppermute(sent, "seqout", [(i, (i + 2 * k) % 8) for i in range(8)])
        out = jnp.where(heads == (x - k) % 4, came[None], out)
    return out


def shards(queries, keys, values, gain, cotangent):
    core = lax.axis_index("seqout") % 2
    x = lax.axis_index("seqout") // 2
    c = core.astype(jnp.int32).reshape(1)
    gain = gain.reshape(1, ROWS)
    aug = (4, AUG, E)
    sums = functools.partial(call, sums_kernel, c, ins=[(keys, "cols"), (values, "cols")], cost=(1 << 25, 1 << 19))
    s_send, f_send = sums(4, 4, outs=[(aug, F32, "step", None)] * 2)
    s_other = swap(s_send)
    s_keep, f_keep = sums(0, 4, outs=[(aug, F32, "step", None)] * 2)
    st = scan(s_keep, s_other, x, False)
    nd_shape = (8, ROWS, 2 * E)
    qkv = [(queries, "cols"), (keys, "cols"), (values, "cols")]
    nd = None
    for start, count in ((0, 3), (3, 3), (6, 2)):
        (nd,) = call(intra_kernel, c, start, count, qkv, [(nd_shape, F32, "at", nd)], cost=(1 << 28, 1 << 21))
    st_keep = st + jnp.where(core == 1, s_other, 0.0)
    st_send = swap(st + jnp.where(core == 0, s_keep, 0.0))

    acc = pltpu.VMEM((ROWS, E), F32)
    full = (8, ROWS, E)

    def attend(start, state, first):
        return call(
            attn_kernel, c, start, 4,
            [(queries, "cols"), (cotangent, "cols"), (gain, "gain"), (nd, "at"), (state, "step"), (first, "step")],
            [((4, ROWS, E), F32, "step", None), ((4, ROWS, E), F32, "step", None), ((16, E), F32, "whole", None)],
            (acc, acc), (1 << 26, 1 << 22),
        )

    attn_k, inv_k, sums_k = attend(0, st_keep, f_keep)
    attn_s, inv_s, sums_s = attend(4, st_send, f_send)
    local = sums_k + sums_s
    far = [lax.ppermute(local, "head", [(i, (i + k) % 4) for i in range(4)]) for k in (1, 2, 3)]
    whole = local + far[0] + far[1] + far[2]
    scale = lax.rsqrt(whole[:8] / D + 1e-06)
    sc = jnp.concatenate([scale, scale**3 * whole[8:] / D], axis=0)

    def grads(start, attn, inv):
        return call(
            grad_kernel, c, start, 4,
            [(queries, "cols"), (cotangent, "cols"), (gain, "gain"), (sc, "whole"), (attn, "step"), (inv, "step")],
            [((4, ROWS, 2 * E), BF16, "step", None), (aug, F32, "step", None), (aug, F32, "step", None)],
            (acc, acc), (1 << 26, 1 << 22),
        )

    g_s, r_send, l_send = grads(4, attn_s, inv_s)
    r_other = swap(r_send)
    g_k, r_keep, l_keep = grads(0, attn_k, inv_k)
    lt = scan(r_keep, r_other, x, True)
    shape = (ROWS, ROWS)

    def back(start, attn, g, state, first, into):
        return call(
            back_kernel, c, start, 4,
            qkv + [(gain, "gain"), (sc, "whole"), (attn, "step"), (g, "step"), (state, "step"), (first, "step")],
            [(shape, BF16, "cols", into[0]), (shape, BF16, "cols", into[1])] + [((4, ROWS, E), F32, "step", None)] * 2,
            (acc,), (1 << 29, 1 << 22),
        )

    dq, mixed, dk_k, dv_k = back(0, attn_k, g_k, st_keep, f_keep, (None, None))
    dq, mixed, dk_s, dv_s = back(4, attn_s, g_s, st_send, f_send, (dq, mixed))
    lt_keep = lt + jnp.where(core == 0, r_other, 0.0)
    lt_send = swap(lt + jnp.where(core == 1, r_keep, 0.0))

    def final(start, dk, dv, later, last, into):
        return call(
            last_kernel, c, start, 4,
            [(keys, "cols"), (values, "cols"), (dk, "step"), (dv, "step"), (later, "step"), (last, "step")],
            [(shape, BF16, "cols", into[0]), (shape, BF16, "cols", into[1])],
            (), (1 << 26, 1 << 22),
        )

    gk, gv = final(0, dk_k, dv_k, lt_keep, l_keep, (None, None))
    gk, gv = final(4, dk_s, dv_s, lt_send, l_send, (gk, gv))
    return mixed, dq, gk, gv


def solution(mesh):
    rows = P(("seqin", "seqout"), "head")
    return jax.shard_map(
        shards,
        mesh=mesh,
        in_specs=(rows, rows, rows, P("head"), rows),
        out_specs=(rows, rows, rows, rows),
        check_vma=False,
    )
```

```python
import functools

import jax
import jax.numpy as jnp
from jax import lax
from jax.experimental import pallas as pl
from jax.experimental.pallas import tpu as pltpu
from jax.sharding import PartitionSpec as P

E = 128
D = 4096
ROWS = 1024
BLOCK = 512
HALF = 256
AUG = E + 8
F32 = jnp.float32
BF16 = jnp.bfloat16
VMEM_LIMIT = 18 * 1024 * 1024


def phi(x):
    xf = x.astype(F32)
    return jnp.where(xf > 0, xf + 1.0, jnp.exp(jnp.minimum(xf, 0.0))).astype(BF16)


def slope(x):
    xf = x.astype(F32)
    return jnp.where(xf > 0, 1.0, jnp.exp(jnp.minimum(xf, 0.0)))


def split(x):
    hi = x.astype(BF16)
    return hi, (x - hi.astype(F32)).astype(BF16)


def dot(a, b, ca=1, cb=0):
    return lax.dot_general(a, b, (((ca,), (cb,)), ((), ())), preferred_element_type=F32)


def iota(shape, dim):
    return lax.broadcasted_iota(jnp.int32, shape, dim)


def column(row):
    return jnp.transpose(jnp.broadcast_to(row, (E, E)))


def columns(at):
    core = lax.rem(lax.axis_index("seqout"), 2)
    return pl.ds(pl.multiple_of(lax.rem(4 * core + at, 8) * E, E), E)


def wide(at):
    return pl.ds(pl.multiple_of(lax.rem(at, 4) * 2 * E, 2 * E), 2 * E)


def each(count, body):
    def step(j, carry):
        body(j)
        return carry

    lax.fori_loop(0, count, step, 0)


def block_sums(fk, v):
    kv = dot(fk, v, 0, 0)
    z = jnp.sum(fk.astype(F32), axis=0, keepdims=True)
    return jnp.concatenate([kv, jnp.broadcast_to(z, (8, E))], axis=0)


def sums_kernel(
    keys_ref, values_ref, queries_ref, cotangent_ref, q_ref, k_ref, v_ref, ct_ref, nd_ref, g_ref, first_ref, last_ref, mask_ref, sems
):
    copies = []
    for i, (src, dst) in enumerate(((keys_ref, k_ref), (values_ref, v_ref), (queries_ref, q_ref), (cotangent_ref, ct_ref))):
        for b in range(2):
            rows = pl.ds(b * BLOCK, BLOCK)
            copies.append(pltpu.make_async_copy(src.at[rows, :], dst.at[rows, :], sems.at[2 * i + b]))
    for i in (0, 2, 1, 3, 4, 5, 6, 7):
        copies[i].start()
    write_masks(mask_ref)
    for b in range(2):
        rows = pl.ds(b * BLOCK, BLOCK)
        copies[b].wait()
        copies[2 + b].wait()

        def one(j):
            cols = columns(j)
            part = block_sums(phi(k_ref[rows, cols]), v_ref[rows, cols])
            if b == 0:
                first_ref[j] = part
            else:
                last_ref[j] = part

        each(8, one)
    for i in (4, 5, 6, 7):
        copies[i].wait()


def intra_kernel(start, count, sent_ref, q_ref, k_ref, v_ref, ct_ref, nd_ref, g_ref, token_ref):
    token_ref[...] = jnp.zeros_like(token_ref)
    tri = iota((HALF, HALF), 0) >= iota((HALF, HALF), 1)
    ones = jnp.ones((BLOCK, E), BF16)

    def one(j):
        cols = columns(start + j)
        for b in range(2):
            rows = pl.ds(b * BLOCK, BLOCK)
            fq, fk = phi(q_ref[rows, cols]), phi(k_ref[rows, cols])
            va = jnp.concatenate([v_ref[rows, cols], ones], axis=1)
            w00 = jnp.where(tri, dot(fq[:HALF], fk[:HALF], 1, 1), 0.0).astype(BF16)
            w10 = dot(fq[HALF:], fk[:HALF], 1, 1).astype(BF16)
            w11 = jnp.where(tri, dot(fq[HALF:], fk[HALF:], 1, 1), 0.0).astype(BF16)
            nd_ref[start + j, pl.ds(b * BLOCK, HALF), :] = dot(w00, va[:HALF])
            nd_ref[start + j, pl.ds(b * BLOCK + HALF, HALF), :] = dot(jnp.concatenate([w10, w11], axis=1), va)

    each(count, one)


def attn_kernel(start, count, gain_ref, st_ref, first_ref, q_ref, k_ref, v_ref, ct_ref, nd_ref, g_ref, sums_ref, sq_acc, pr_acc):
    sq_acc[...] = jnp.zeros_like(sq_acc)
    pr_acc[...] = jnp.zeros_like(pr_acc)

    def one(j):
        cols = columns(start + j)
        for b in range(2):
            rows = pl.ds(b * BLOCK, BLOCK)
            aug = st_ref[j] + first_ref[start + j] if b else st_ref[j]
            s_hi, s_lo = split(aug[:E])
            n_hi, n_lo = split(column(aug[E : E + 1]))
            rhs = jnp.concatenate([jnp.concatenate([s_hi, n_hi], axis=1), jnp.concatenate([s_lo, n_lo], axis=1)], axis=0)
            fq = phi(q_ref[rows, cols])
            nd = nd_ref[start + j, rows, :] + dot(jnp.concatenate([fq, fq], axis=1), rhs)
            inv = 1.0 / nd[:, E:]
            attn = nd[:, :E] * inv
            nd_ref[start + j, rows, :] = jnp.concatenate([attn, inv], axis=1)
            sq_acc[rows, :] += attn * attn
            pr_acc[rows, :] += ct_ref[rows, cols].astype(F32) * gain_ref[:, cols] * attn

    each(count, one)
    for i in range(8):
        rows = pl.ds(i * E, E)
        sums_ref[pl.ds(i, 1), :] = jnp.sum(jnp.transpose(sq_acc[rows, :]), axis=0, keepdims=True)
        sums_ref[pl.ds(8 + i, 1), :] = jnp.sum(jnp.transpose(pr_acc[rows, :]), axis=0, keepdims=True)


def spread(sc_ref, scale_ref, coef_ref):
    for i in range(8):
        rows = pl.ds(i * E, E)
        scale_ref[rows, :] = column(sc_ref[pl.ds(i, 1), :])
        if coef_ref is not None:
            coef_ref[rows, :] = column(sc_ref[pl.ds(8 + i, 1), :])


def grad_kernel(start, count, gain_ref, sc_ref, q_ref, k_ref, v_ref, ct_ref, nd_ref, g_ref, first_ref, last_ref, scale_ref, coef_ref):
    spread(sc_ref, scale_ref, coef_ref)
    lane = iota((BLOCK, E), 1)
    ones = jnp.ones((2 * E, E), BF16)

    def one(j):
        cols = columns(start + j)
        for b in range(2):
            rows = pl.ds(b * BLOCK, BLOCK)
            attn, inv = nd_ref[start + j, rows, :E], nd_ref[start + j, rows, E:]
            weighted = ct_ref[rows, cols].astype(F32) * gain_ref[:, cols]
            d_attn = scale_ref[rows, :] * weighted - attn * coef_ref[rows, :]
            g = (d_attn * inv).astype(BF16)
            p_hi, p_lo = split(d_attn * attn)
            gd = -dot(jnp.concatenate([p_hi, p_lo], axis=1), ones) * inv
            gd_hi, gd_lo = split(gd)
            aug = jnp.where((lane == 0) | (lane == 2), gd_hi, jnp.where(lane == 1, gd_lo, jnp.zeros_like(gd_lo)))
            g_ref.at[lax.div(start + j, 4)][rows, wide(start + j)] = jnp.concatenate([g, aug], axis=1)
            fq = phi(q_ref[rows, cols])
            rev = dot(fq, g, 0, 0)
            rden = jnp.sum(gd * fq.astype(F32), axis=0, keepdims=True)
            part = jnp.concatenate([rev, jnp.broadcast_to(rden, (8, E))], axis=0)
            if b == 0:
                first_ref[j] = part
            else:
                last_ref[j] = part

    each(count, one)


def back_kernel(
    start, count, gain_ref, sc_ref, st_ref, first_ref, sent_ref, q_ref, k_ref, v_ref, ct_ref, nd_ref, g_ref,
    dq_ref, mixed_ref, token_ref, scale_ref, dq_buf, mixed_buf, sems,
):
    token_ref[...] = jnp.zeros_like(token_ref)
    spread(sc_ref, scale_ref, None)
    low = iota((HALF, HALF), 0) >= iota((HALF, HALF), 1)
    up = iota((HALF, HALF), 0) <= iota((HALF, HALF), 1)
    flag = jnp.where(iota((BLOCK, E), 1) < 2, 1.0, 0.0).astype(BF16)
    lane = iota((E, E), 1)

    def copies(j):
        cols = columns(start + j)
        return [
            pltpu.make_async_copy(dq_buf.at[j], dq_ref.at[:, cols], sems.at[0, j]),
            pltpu.make_async_copy(mixed_buf.at[j], mixed_ref.at[:, cols], sems.at[1, j]),
        ]

    def one(j):
        cols = columns(start + j)
        for b in range(2):
            rows = pl.ds(b * BLOCK, BLOCK)
            q, v = q_ref[rows, cols], v_ref[rows, cols]
            fq, fk = phi(q), phi(k_ref[rows, cols])
            ga = g_ref.at[lax.div(start + j, 4)][rows, wide(start + j)]
            g = ga[:, :E]
            va = jnp.concatenate([v, flag], axis=1)
            m00 = jnp.where(low, dot(ga[:HALF], va[:HALF], 1, 1), 0.0).astype(BF16)
            m10 = dot(ga[HALF:], va[:HALF], 1, 1).astype(BF16)
            m11 = jnp.where(low, dot(ga[HALF:], va[HALF:], 1, 1), 0.0).astype(BF16)
            w00 = jnp.where(up, dot(fk[:HALF], fq[:HALF], 1, 1), 0.0).astype(BF16)
            w10 = dot(fk[:HALF], fq[HALF:], 1, 1).astype(BF16)
            w11 = jnp.where(up, dot(fk[HALF:], fq[HALF:], 1, 1), 0.0).astype(BF16)
            at = start % 4 + j
            aug = st_ref[at] + first_ref[start + j] if b else st_ref[at]
            s_hi, s_lo = split(aug[:E])
            n_hi, n_lo = split(column(aug[E : E + 1]))
            naug = jnp.where(lane < 2, n_hi, jnp.where(lane == 2, n_lo, jnp.zeros_like(n_lo)))
            rhs = jnp.concatenate([s_hi, s_lo, naug], axis=1)
            dfq = dot(jnp.concatenate([g, ga], axis=1), rhs, 1, 1)
            dfq = dfq + jnp.concatenate([dot(m00, fk[:HALF]), dot(jnp.concatenate([m10, m11], axis=1), fk)], axis=0)
            dq_buf[j, rows, :] = (dfq * slope(q)).astype(BF16)
            mixed_buf[j, rows, :] = (nd_ref[start + j, rows, :E] * scale_ref[rows, :] * gain_ref[:, cols]).astype(BF16)
            nd_ref[start + j, pl.ds(b * BLOCK, HALF), :E] = dot(jnp.concatenate([m00, m10], axis=0), fq, 0, 0)
            nd_ref[start + j, pl.ds(b * BLOCK + HALF, HALF), :E] = dot(m11, fq[HALF:], 0, 0)
            nd_ref[start + j, pl.ds(b * BLOCK, HALF), E:] = dot(jnp.concatenate([w00, w10], axis=1), g)
            nd_ref[start + j, pl.ds(b * BLOCK + HALF, HALF), E:] = dot(w11, g[HALF:])
        for copy in copies(j):
            copy.start()

    each(count, one)
    for j in range(count):
        for copy in copies(j):
            copy.wait()


def last_kernel(start, count, lt_ref, last_ref, q_ref, k_ref, v_ref, ct_ref, nd_ref, g_ref, gk_ref, gv_ref, gk_buf, gv_buf, sems):

    def copies(j):
        cols = columns(start + j)
        return [
            pltpu.make_async_copy(gk_buf.at[j], gk_ref.at[:, cols], sems.at[0, j]),
            pltpu.make_async_copy(gv_buf.at[j], gv_ref.at[:, cols], sems.at[1, j]),
        ]

    def one(j):
        cols = columns(start + j)
        for b in range(2):
            rows = pl.ds(b * BLOCK, BLOCK)
            k, v = k_ref[rows, cols], v_ref[rows, cols]
            fk = phi(k)
            aug = lt_ref[j] if b else lt_ref[j] + last_ref[start + j]
            l_hi, l_lo = split(aug[:E])
            dfk = dot(jnp.concatenate([v, v], axis=1), jnp.concatenate([l_hi, l_lo], axis=1), 1, 1)
            dfk = dfk + nd_ref[start + j, rows, :E] + aug[E : E + 1]
            dv = dot(jnp.concatenate([fk, fk], axis=1), jnp.concatenate([l_hi, l_lo], axis=0))
            gk_buf[j, rows, :] = (dfk * slope(k)).astype(BF16)
            gv_buf[j, rows, :] = (dv + nd_ref[start + j, rows, E:]).astype(BF16)
        for copy in copies(j):
            copy.start()

    each(count, one)
    for j in range(count):
        for copy in copies(j):
            copy.wait()


def vmem(shape, dtype=F32, into=None):
    return pltpu.VMEM(shape, dtype), into


def hbm(shape, dtype, into=None):
    return pltpu.HBM(shape, dtype), into


def call(kernel, near, far, outs, scratch=(), flops=0):
    arrays = [pltpu.with_memory_space_constraint(a, pltpu.VMEM) for a in near]
    arrays += far
    specs = [pl.BlockSpec(memory_space=pltpu.VMEM)] * len(near) + [pl.BlockSpec(memory_space=pl.ANY)] * len(far)
    first, shapes, out_specs, aliases = len(arrays), [], [], {}
    for i, (shape, into) in enumerate(outs):
        space = pl.ANY if shape.memory_space == pltpu.HBM else pltpu.VMEM
        shapes.append(shape)
        out_specs.append(pl.BlockSpec(memory_space=space))
        if into is not None:
            aliases[len(arrays)] = i
            arrays.append(pltpu.with_memory_space_constraint(into, shape.memory_space))
            specs.append(pl.BlockSpec(memory_space=space))

    def body(*refs):
        bank, nd, *own = refs[len(arrays) :]
        kernel(*refs[:first], *(bank.at[i] for i in range(4)), nd, bank.at[pl.ds(4, 2)], *own)

    return pl.pallas_call(
        body,
        out_shape=shapes,
        in_specs=specs,
        out_specs=out_specs,
        scratch_shapes=list(scratch),
        input_output_aliases=aliases,
        compiler_params=pltpu.CompilerParams(vmem_limit_bytes=VMEM_LIMIT),
        cost_estimate=pl.CostEstimate(flops=flops, bytes_accessed=1 << 20, transcendentals=0),
    )(*arrays)


CORE = [(i, i ^ 1) for i in range(8)]


def swap(x):
    return lax.ppermute(x, "seqout", CORE)


TO, SOURCE, BEFORE, AFTER, LOWER, UPPER, MASKS = 0, 16, 32, 48, 64, 65, 72


def write_masks(mask_ref):
    place = lax.axis_index("seqout")
    x, core = lax.div(place, 2), lax.rem(place, 2)

    def put(at, true):
        mask_ref[pl.ds(at, 1), :] = jnp.full((1, E), jnp.where(true, 1.0, 0.0), F32)

    for k in range(4):
        to = lax.rem(x + k, 4)
        for i in range(4):
            source = lax.rem(x + 4 - i, 4)
            put(TO + 4 * k + i, to == i)
            put(SOURCE + 4 * k + i, lax.rem(x + 4 - k, 4) == i)
            put(BEFORE + 4 * k + i, source < to)
            put(AFTER + 4 * k + i, source > to)
    put(LOWER, core == 0)
    put(UPPER, core == 1)


def keep_where(mask, at, x):
    return jnp.where(mask[at : at + 1] > 0, x, 0.0)


def add(parts):
    return functools.reduce(lambda a, b: a + b, parts)


def scan(sums, mask, reverse, during):
    other = swap(sums[4:])
    total = sums[:4] + other + during[0](sums)
    got = [add([keep_where(mask, TO + 4 * k + h, total[h]) for h in range(4)]) for k in range(4)]
    own = got[0]
    for k in (1, 2, 3):
        got[k] = lax.ppermute(got[k], "seqout", [(i, (i + 2 * k) % 8) for i in range(8)])
    row = got[0] + got[1] + got[2] + got[3] + during[1](own)
    rows = []
    for k in (1, 2, 3):
        pairs = [(i, i - k) if reverse else (i, i + k) for i in range(4)]
        rows.append(lax.ppermute(row, "seqin", [(a, b) for a, b in pairs if 0 <= b < 4]))
    base = rows[0] + rows[1] + rows[2] + during[2](row)
    at = AFTER if reverse else BEFORE
    came = [base + add([keep_where(mask, at + 4 * k + m, got[m]) for m in range(4)]) for k in range(4)]
    for k in (1, 2, 3):
        came[k] = lax.ppermute(came[k], "seqout", [(i, (i + 2 * k) % 8) for i in range(8)])
    zeros = during[3](base)
    out = [add([keep_where(mask, SOURCE + 4 * k + h, came[k]) for k in range(4)]) + zeros for h in range(4)]
    return jnp.stack(out), other


def shards(queries, keys, values, gain, cotangent):
    gain = gain.reshape(1, ROWS)
    shape = (ROWS, ROWS)
    aug = vmem((4, AUG, E))
    token = vmem((8, E))
    acc = pltpu.VMEM((ROWS, E), F32)
    sems = pltpu.SemaphoreType.DMA
    kept = {}
    sizes = {"bank": ((6, ROWS, ROWS), BF16), "nd": ((8, ROWS, 2 * E), F32)}

    def run(kernel, near, far, outs, scratch=(), flops=0):
        held = [vmem(*size, kept.get(name)) for name, size in sizes.items()]
        got = call(kernel, near, [pltpu.with_memory_space_constraint(a, pltpu.HBM) if a.shape == shape else a for a in far], held + outs, scratch, flops)
        kept.update(zip(sizes, got))
        return got[len(sizes) :]

    parts = vmem((8, AUG, E))
    far = [keys, values, queries, cotangent]
    first, last, mask = run(sums_kernel, [], far, [parts, parts, vmem((MASKS, E))], [sems((8,))], 1 << 28)
    sums = first + last

    def intra(start, count):
        def during(sent):
            kernel = functools.partial(intra_kernel, start, count)
            (zeros,) = run(kernel, [], [sent], [token], (), count << 28)
            return zeros[:1]

        return during

    st, other = scan(sums, mask, False, (intra(0, 2), intra(2, 2), intra(4, 2), intra(6, 2)))
    st_keep = st + keep_where(mask, UPPER, other)
    st_send = swap(st + keep_where(mask, LOWER, sums[:4]))

    def attend(start, state):
        kernel = functools.partial(attn_kernel, start, 4)
        near = [gain, state, first]
        return run(kernel, near, [], [vmem((16, E))], (acc, acc), 1 << 28)[0]

    local = attend(0, st_keep)
    local = local + attend(4, st_send)
    far = [lax.ppermute(local, "head", [(i, (i + k) % 4) for i in range(4)]) for k in (1, 2, 3)]
    whole = local + far[0] + far[1] + far[2]
    scale = lax.rsqrt(whole[:8] / D + 1e-06)
    sc = jnp.concatenate([scale, scale**3 * whole[8:] / D], axis=0)

    kernel = functools.partial(grad_kernel, 0, 8)
    back_first, back_last = run(kernel, [gain, sc], [], [parts, parts], (acc, acc), 1 << 29)
    back_sums = back_first + back_last
    dq = mixed = None

    def back(start, count):
        def during(sent):
            nonlocal dq, mixed
            state = st_send if start >= 4 else st_keep
            out = pltpu.VMEM((count, ROWS, E), BF16)
            dq, mixed, zeros = run(
                functools.partial(back_kernel, start, count),
                [gain, sc, state, first], [sent], [hbm(shape, BF16, dq), hbm(shape, BF16, mixed), token],
                (acc, out, out, sems((2, count))), count << 29,
            )
            return zeros[:1]

        return during

    lt, other = scan(back_sums, mask, True, (back(0, 2), back(2, 2), back(4, 2), back(6, 2)))
    lt_keep = lt + keep_where(mask, LOWER, other)
    lt_send = swap(lt + keep_where(mask, UPPER, back_sums[:4]))
    gk = gv = None
    for start, later in ((0, lt_keep), (4, lt_send)):
        out = pltpu.VMEM((4, ROWS, E), BF16)
        gk, gv = run(
            functools.partial(last_kernel, start, 4), [later, back_last], [],
            [hbm(shape, BF16, gk), hbm(shape, BF16, gv)], (out, out, sems((2, 4))), 1 << 28,
        )
    return mixed, dq, gk, gv


def solution(mesh):
    rows = P(("seqin", "seqout"), "head")
    return jax.shard_map(
        shards,
        mesh=mesh,
        in_specs=(rows, rows, rows, P("head"), rows),
        out_specs=(rows, rows, rows, rows),
        check_vma=False,
    )
```

```python
import functools

import jax
import jax.numpy as jnp
from jax import lax
from jax.experimental import pallas as pl
from jax.experimental.pallas import tpu as pltpu
from jax.sharding import PartitionSpec as P

E = 128
D = 4096
ROWS = 1024
BLOCK = 512
HALF = 256
AUG = E + 8
F32 = jnp.float32
BF16 = jnp.bfloat16
VMEM_LIMIT = 16 * 1024 * 1024
UNROLL = 2
ORDER = (2, 1, 3)
USE = (0, 2, 1, 3)
ROW_ORDER = (1, 3, 2)


def phi(x):
    xf = x.astype(F32)
    return jnp.where(xf > 0, xf + 1.0, jnp.exp(xf)).astype(BF16)


def slope(x):
    xf = x.astype(F32)
    return jnp.where(xf > 0, 1.0, jnp.exp(xf))


def split(x):
    hi = x.astype(BF16)
    return hi, (x - hi.astype(F32)).astype(BF16)


def dot(a, b, ca=1, cb=0):
    return lax.dot_general(a, b, (((ca,), (cb,)), ((), ())), preferred_element_type=F32)


def iota(shape, dim):
    return lax.broadcasted_iota(jnp.int32, shape, dim)


def column(row):
    return jnp.transpose(jnp.broadcast_to(row, (E, E)))


def columns(at):
    core = lax.rem(lax.axis_index("seqout"), 2)
    return pl.ds(pl.multiple_of(lax.rem(4 * core + at, 8) * E, E), E)


def each(count, body):
    def step(j, carry):
        body(j)
        return carry

    lax.fori_loop(0, count, step, 0, unroll=UNROLL)


def block_sums(fk, v):
    kv = dot(fk, v, 0, 0)
    z = jnp.sum(fk.astype(F32), axis=0, keepdims=True)
    return jnp.concatenate([kv, jnp.broadcast_to(z, (8, E))], axis=0)


def sums_kernel(
    keys_ref, values_ref, queries_ref, cotangent_ref, q_ref, k_ref, v_ref, ct_ref, fq_ref, fk_ref, nd_ref, gr_ref, g_ref, first_ref, last_ref, mask_ref, sems
):
    half = ROWS // 2
    near = pl.ds(pl.multiple_of(half * lax.rem(lax.axis_index("seqout"), 2), half), half)
    away = pl.ds(pl.multiple_of(half - half * lax.rem(lax.axis_index("seqout"), 2), half), half)
    top, bottom = pl.ds(0, BLOCK), pl.ds(BLOCK, BLOCK)
    copies = []
    for at in ((top, near), (top, away), (bottom, slice(None))):
        for src, dst in ((keys_ref, k_ref), (values_ref, v_ref)):
            copies.append(pltpu.make_async_copy(src.at[at], dst.at[at], sems.at[len(copies)]))
    for src, dst in ((queries_ref, q_ref), (cotangent_ref, ct_ref)):
        copies.append(pltpu.make_async_copy(src, dst, sems.at[len(copies)]))
    for copy in copies:
        copy.start()
    write_masks(mask_ref)
    for step in range(4):
        b = step // 2
        rows = pl.ds(b * BLOCK, BLOCK)
        if step < 3:
            copies[2 * step].wait()
            copies[2 * step + 1].wait()

        def group(i):
            done = []
            for j in (4 * (step % 2) + 2 * i, 4 * (step % 2) + 2 * i + 1):
                cols = columns(j)
                fk = phi(k_ref[rows, cols])
                done.append((j, cols, fk, block_sums(fk, v_ref[rows, cols])))
            for j, cols, fk, part in done:
                fk_ref[rows, cols] = fk
                (last_ref if b else first_ref)[j] = part

        each(2, group)
    for copy in copies[6:]:
        copy.wait()


def intra_kernel(start, count, sent_ref, q_ref, k_ref, v_ref, ct_ref, fq_ref, fk_ref, nd_ref, gr_ref, g_ref, token_ref):
    token_ref[...] = jnp.zeros_like(token_ref)
    tri = iota((HALF, HALF), 0) >= iota((HALF, HALF), 1)
    ones = jnp.ones((BLOCK, E), BF16)

    def one(j):
        cols = columns(start + j)
        done = []
        for b in range(2):
            rows = pl.ds(b * BLOCK, BLOCK)
            fq, fk = phi(q_ref[rows, cols]), fk_ref[rows, cols]
            done.append((rows, fq))
            va = jnp.concatenate([v_ref[rows, cols], ones], axis=1)
            w00 = jnp.where(tri, dot(fq[:HALF], fk[:HALF], 1, 1), 0.0).astype(BF16)
            w10 = dot(fq[HALF:], fk[:HALF], 1, 1).astype(BF16)
            w11 = jnp.where(tri, dot(fq[HALF:], fk[HALF:], 1, 1), 0.0).astype(BF16)
            nd_ref[start + j, pl.ds(b * BLOCK, HALF), :] = dot(w00, va[:HALF])
            nd_ref[start + j, pl.ds(b * BLOCK + HALF, HALF), :] = dot(jnp.concatenate([w10, w11], axis=1), va)
        for rows, fq in done:
            fq_ref[rows, cols] = fq

    each(count, one)


def attn_kernel(start, count, gain_ref, st_ref, first_ref, q_ref, k_ref, v_ref, ct_ref, fq_ref, fk_ref, nd_ref, gr_ref, g_ref, sums_ref, sq_acc, pr_acc):
    sq_acc[...] = jnp.zeros_like(sq_acc)
    pr_acc[...] = jnp.zeros_like(pr_acc)

    def pair(i):
        for b in range(2):
            rows = pl.ds(b * BLOCK, BLOCK)
            squares, products = [], []
            for j in (2 * i, 2 * i + 1):
                cols = columns(start + j)
                aug = st_ref[j] + first_ref[start + j] if b else st_ref[j]
                s_hi, s_lo = split(aug[:E])
                n_hi, n_lo = split(column(aug[E : E + 1]))
                rhs = jnp.concatenate([jnp.concatenate([s_hi, n_hi], axis=1), jnp.concatenate([s_lo, n_lo], axis=1)], axis=0)
                fq = fq_ref[rows, cols]
                nd = nd_ref[start + j, rows, :] + dot(jnp.concatenate([fq, fq], axis=1), rhs)
                inv = 1.0 / nd[:, E:]
                attn = nd[:, :E] * inv
                nd_ref[start + j, rows, :] = jnp.concatenate([attn, inv], axis=1)
                squares.append(attn * attn)
                products.append(ct_ref[rows, cols].astype(F32) * gain_ref[:, cols] * attn)
            sq_acc[rows, :] += squares[0] + squares[1]
            pr_acc[rows, :] += products[0] + products[1]

    each(count // 2, pair)
    for i in range(8):
        rows = pl.ds(i * E, E)
        sums_ref[pl.ds(i, 1), :] = jnp.sum(jnp.transpose(sq_acc[rows, :]), axis=0, keepdims=True)
        sums_ref[pl.ds(8 + i, 1), :] = jnp.sum(jnp.transpose(pr_acc[rows, :]), axis=0, keepdims=True)


def spread(sc_ref, scale_ref, coef_ref):
    for i in range(8):
        rows = pl.ds(i * E, E)
        scale_ref[rows, :] = column(sc_ref[pl.ds(i, 1), :])
        if coef_ref is not None:
            coef_ref[rows, :] = column(sc_ref[pl.ds(8 + i, 1), :])


def rows_kernel(gain_ref, sent_ref, q_ref, k_ref, v_ref, ct_ref, fq_ref, fk_ref, nd_ref, gr_ref, g_ref, p_ref, s_ref):
    ones = jnp.ones((8, 2 * E), BF16)

    def row_sums(x):
        hi, lo = split(x)
        return dot(ones, jnp.concatenate([hi, lo], axis=1), 1, 1)[0:1]

    def one(j):
        cols = columns(j)
        for b in range(2):
            rows = pl.ds(b * BLOCK, BLOCK)
            attn, inv = nd_ref[j, rows, :E], nd_ref[j, rows, E:]
            wi = ct_ref[rows, cols].astype(F32) * gain_ref[:, cols] * inv
            ai = attn * inv
            p, s = row_sums(wi * attn), row_sums(ai * attn)
            gr_ref[j, rows, :] = wi
            nd_ref[j, rows, E:] = ai
            for i in range(4):
                p_ref[j, pl.ds(4 * b + i, 1), :] = p[:, i * E : (i + 1) * E]
                s_ref[j, pl.ds(4 * b + i, 1), :] = s[:, i * E : (i + 1) * E]

    each(8, one)


def grad_kernel(
    gain_ref, sc_ref, p_ref, s_ref, q_ref, k_ref, v_ref, ct_ref, fq_ref, fk_ref, nd_ref, gr_ref, g_ref, first_ref, last_ref, gd_ref, scale_ref, coef_ref
):
    spread(sc_ref, scale_ref, coef_ref)

    def group(i):
        done = []
        for j in (2 * i, 2 * i + 1):
            cols = columns(j)
            gd = sc_ref[8:16, :] * s_ref[j] - sc_ref[0:8, :] * p_ref[j]
            hi = gd.astype(BF16).astype(F32)
            for b in range(2):
                rows = pl.ds(b * BLOCK, BLOCK)
                g = (scale_ref[rows, :] * gr_ref[j, rows, :] - coef_ref[rows, :] * nd_ref[j, rows, E:]).astype(BF16)
                pieces = [jnp.concatenate([x[4 * b + i : 4 * b + i + 1] for i in range(4)], axis=1) for x in (hi, gd - hi)]
                pieces.append(jnp.zeros((14, BLOCK), F32))
                fq = fq_ref[rows, cols]
                rden = dot(jnp.concatenate(pieces, axis=0).astype(BF16), fq)
                rden = jnp.broadcast_to(rden[0:1] + rden[1:2], (8, E))
                done.append((j, b, rows, g, jnp.concatenate([dot(fq, g, 0, 0), rden], axis=0)))
            gd_ref[j] = gd
        for j, b, rows, g, part in done:
            g_ref[rows, pl.ds(pl.multiple_of(j * E, E), E)] = g
            (last_ref if b else first_ref)[j] = part

    each(4, group)


def back_kernel(
    start, count, gain_ref, sc_ref, st_ref, first_ref, gd_ref, sent_ref, q_ref, k_ref, v_ref, ct_ref, fq_ref, fk_ref, nd_ref, gr_ref, g_ref,
    dq_ref, mixed_ref, token_ref, scale_ref, dq_buf, mixed_buf, sems,
):
    token_ref[...] = jnp.zeros_like(token_ref)
    spread(sc_ref, scale_ref, None)
    low = iota((HALF, HALF), 0) >= iota((HALF, HALF), 1)
    up = iota((HALF, HALF), 0) <= iota((HALF, HALF), 1)

    def copies(j):
        cols = columns(start + j)
        return [
            pltpu.make_async_copy(dq_buf.at[j], dq_ref.at[:, cols], sems.at[0, j]),
            pltpu.make_async_copy(mixed_buf.at[j], mixed_ref.at[:, cols], sems.at[1, j]),
        ]

    def one(j):
        cols = columns(start + j)
        for b in range(2):
            rows = pl.ds(b * BLOCK, BLOCK)
            v, fq, fk = v_ref[rows, cols], fq_ref[rows, cols], fk_ref[rows, cols]
            g = g_ref[rows, pl.ds(pl.multiple_of((start + j) * E, E), E)]
            gd = jnp.concatenate([column(gd_ref[start + j, pl.ds(4 * b + i, 1), :]) for i in range(4)], axis=0)
            add0, add1 = (jnp.concatenate([x, x], axis=1) for x in (gd[:HALF], gd[HALF:]))
            m00 = jnp.where(low, dot(g[:HALF], v[:HALF], 1, 1) + add0, 0.0).astype(BF16)
            m10 = (dot(g[HALF:], v[:HALF], 1, 1) + add1).astype(BF16)
            m11 = jnp.where(low, dot(g[HALF:], v[HALF:], 1, 1) + add1, 0.0).astype(BF16)
            w00 = jnp.where(up, dot(fk[:HALF], fq[:HALF], 1, 1), 0.0).astype(BF16)
            w10 = dot(fk[:HALF], fq[HALF:], 1, 1).astype(BF16)
            w11 = jnp.where(up, dot(fk[HALF:], fq[HALF:], 1, 1), 0.0).astype(BF16)
            at = start % 4 + j
            aug = st_ref[at] + first_ref[start + j] if b else st_ref[at]
            s_hi, s_lo = split(aug[:E])
            rhs = jnp.concatenate([s_hi, s_lo], axis=1)
            dfq = dot(jnp.concatenate([g, g], axis=1), rhs, 1, 1) + gd * aug[E : E + 1]
            dfq = dfq + jnp.concatenate([dot(m00, fk[:HALF]), dot(jnp.concatenate([m10, m11], axis=1), fk)], axis=0)
            dq_buf[j, rows, :] = (dfq * slope(q_ref[rows, cols])).astype(BF16)
            mixed_buf[j, rows, :] = (nd_ref[start + j, rows, :E] * scale_ref[rows, :] * gain_ref[:, cols]).astype(BF16)
            nd_ref[start + j, pl.ds(b * BLOCK, HALF), :E] = dot(jnp.concatenate([m00, m10], axis=0), fq, 0, 0)
            nd_ref[start + j, pl.ds(b * BLOCK + HALF, HALF), :E] = dot(m11, fq[HALF:], 0, 0)
            nd_ref[start + j, pl.ds(b * BLOCK, HALF), E:] = dot(jnp.concatenate([w00, w10], axis=1), g)
            nd_ref[start + j, pl.ds(b * BLOCK + HALF, HALF), E:] = dot(w11, g[HALF:])
        for copy in copies(j):
            copy.start()

    each(count, one)
    for j in range(count):
        for copy in copies(j):
            copy.wait()


def last_kernel(start, count, lt_ref, last_ref, q_ref, k_ref, v_ref, ct_ref, fq_ref, fk_ref, nd_ref, gr_ref, g_ref, gk_ref, gv_ref, gk_buf, gv_buf, sems):

    def copies(j):
        cols = columns(start + j)
        return [
            pltpu.make_async_copy(gk_buf.at[j], gk_ref.at[:, cols], sems.at[0, j]),
            pltpu.make_async_copy(gv_buf.at[j], gv_ref.at[:, cols], sems.at[1, j]),
        ]

    def group(i):
        for j in (2 * i, 2 * i + 1):
            cols = columns(start + j)
            for b in range(2):
                rows = pl.ds(b * BLOCK, BLOCK)
                v, fk = v_ref[rows, cols], fk_ref[rows, cols]
                aug = lt_ref[j] if b else lt_ref[j] + last_ref[start + j]
                l_hi, l_lo = split(aug[:E])
                dfk = dot(jnp.concatenate([v, v], axis=1), jnp.concatenate([l_hi, l_lo], axis=1), 1, 1)
                dfk = dfk + nd_ref[start + j, rows, :E] + aug[E : E + 1]
                dv = dot(jnp.concatenate([fk, fk], axis=1), jnp.concatenate([l_hi, l_lo], axis=0))
                gk_buf[j, rows, :] = (dfk * slope(k_ref[rows, cols])).astype(BF16)
                gv_buf[j, rows, :] = (dv + nd_ref[start + j, rows, E:]).astype(BF16)
        for j in (2 * i, 2 * i + 1):
            for copy in copies(j):
                copy.start()

    for i in range(count // 2):
        group(i)
    for j in range(count):
        for copy in copies(j):
            copy.wait()


def vmem(shape, dtype=F32, into=None):
    return pltpu.VMEM(shape, dtype), into


def hbm(shape, dtype, into=None):
    return pltpu.HBM(shape, dtype), into


def call(kernel, near, far, outs, scratch=(), flops=0):
    arrays = [pltpu.with_memory_space_constraint(a, pltpu.VMEM) for a in near]
    arrays += far
    specs = [pl.BlockSpec(memory_space=pltpu.VMEM)] * len(near) + [pl.BlockSpec(memory_space=pl.ANY)] * len(far)
    first, shapes, out_specs, aliases = len(arrays), [], [], {}
    for i, (shape, into) in enumerate(outs):
        space = pl.ANY if shape.memory_space == pltpu.HBM else pltpu.VMEM
        shapes.append(shape)
        out_specs.append(pl.BlockSpec(memory_space=space))
        if into is not None:
            aliases[len(arrays)] = i
            arrays.append(pltpu.with_memory_space_constraint(into, shape.memory_space))
            specs.append(pl.BlockSpec(memory_space=space))

    def body(*refs):
        bank, nd, gr, *own = refs[len(arrays) :]
        kernel(*refs[:first], *(bank.at[i] for i in range(6)), nd, gr, bank.at[6], *own)

    return pl.pallas_call(
        body,
        out_shape=shapes,
        in_specs=specs,
        out_specs=out_specs,
        scratch_shapes=list(scratch),
        input_output_aliases=aliases,
        compiler_params=pltpu.CompilerParams(vmem_limit_bytes=VMEM_LIMIT),
        cost_estimate=pl.CostEstimate(flops=flops, bytes_accessed=1 << 20, transcendentals=0),
    )(*arrays)


CORE = [(i, i ^ 1) for i in range(8)]


def send_x(x, k):
    return lax.ppermute(x, "seqout", [(i, (i + 2 * k) % 8) for i in range(8)])


def send_y(x, k):
    return lax.ppermute(x, "seqin", [(i, (i + k) % 4) for i in range(4)])


def swap(x):
    return lax.ppermute(x, "seqout", CORE)


TO, SOURCE, BEFORE, AFTER, LOWER, UPPER, ROW_BEFORE, ROW_AFTER, MASKS = 0, 16, 32, 48, 64, 65, 66, 70, 80


def write_masks(mask_ref):
    place = lax.axis_index("seqout")
    x, core = lax.div(place, 2), lax.rem(place, 2)

    def put(at, true):
        mask_ref[pl.ds(at, 1), :] = jnp.full((1, E), jnp.where(true, 1.0, 0.0), F32)

    for k in range(4):
        to = lax.rem(x + k, 4)
        for i in range(4):
            source = lax.rem(x + 4 - i, 4)
            put(TO + 4 * k + i, to == i)
            put(SOURCE + 4 * k + i, lax.rem(x + 4 - k, 4) == i)
            put(BEFORE + 4 * k + i, source < to)
            put(AFTER + 4 * k + i, source > to)
    y = lax.axis_index("seqin")
    for k in range(4):
        put(ROW_BEFORE + k, y >= k)
        put(ROW_AFTER + k, y < 4 - k)
    put(LOWER, core == 0)
    put(UPPER, core == 1)


def keep_where(mask, at, x):
    return jnp.where(mask[at : at + 1] > 0, x, 0.0)


def add(parts):
    return functools.reduce(lambda a, b: a + b, parts)


def scan(sums, mask, reverse, during):
    other = swap(sums[4:])
    total = sums[:4] + other + during[0](sums)
    got = {k: add([keep_where(mask, TO + 4 * k + h, total[h]) for h in range(4)]) for k in (*ORDER, 0)}
    own = got[0]
    for k in ORDER:
        got[k] = send_x(got[k], k)
    row = add([got[k] for k in USE]) + during[1](own)
    rows = []
    for k in ROW_ORDER:
        came = send_y(row, -k if reverse else k)
        rows.append(keep_where(mask, (ROW_AFTER if reverse else ROW_BEFORE) + k, came))
    base = rows[0] + rows[1] + rows[2] + during[2](row)
    at = AFTER if reverse else BEFORE
    came = {k: base + add([keep_where(mask, at + 4 * k + m, got[m]) for m in USE]) for k in (*ORDER, 0)}
    for k in ORDER:
        came[k] = send_x(came[k], k)
    zeros = during[3](base)
    out = [add([keep_where(mask, SOURCE + 4 * k + h, came[k]) for k in USE]) + zeros for h in range(4)]
    return jnp.stack(out), other


def shards(queries, keys, values, gain, cotangent):
    gain = gain.reshape(1, ROWS)
    shape = (ROWS, ROWS)
    aug = vmem((4, AUG, E))
    token = vmem((8, E))
    acc = pltpu.VMEM((ROWS, E), F32)
    sems = pltpu.SemaphoreType.DMA
    kept = {}
    sizes = {"bank": ((7, ROWS, ROWS), BF16), "nd": ((8, ROWS, 2 * E), F32), "gr": ((8, ROWS, E), F32)}

    def run(kernel, near, far, outs, scratch=(), flops=0):
        held = [vmem(*size, kept.get(name)) for name, size in sizes.items()]
        got = call(kernel, near, [pltpu.with_memory_space_constraint(a, pltpu.HBM) if a.shape == shape else a for a in far], held + outs, scratch, flops)
        kept.update(zip(sizes, got))
        return got[len(sizes) :]

    parts = vmem((8, AUG, E))
    far = [keys, values, queries, cotangent]
    first, last, mask = run(sums_kernel, [], far, [parts, parts, vmem((MASKS, E))], [sems((8,))], 1 << 28)
    sums = first + last

    def intra(start, count):
        def during(sent):
            kernel = functools.partial(intra_kernel, start, count)
            (zeros,) = run(kernel, [], [sent], [token], (), count << 28)
            return zeros[:1]

        return during

    st, other = scan(sums, mask, False, (intra(0, 2), intra(2, 2), intra(4, 2), intra(6, 2)))
    st_keep = st + keep_where(mask, UPPER, other)
    st_send = swap(st + keep_where(mask, LOWER, sums[:4]))

    def attend(start, state):
        kernel = functools.partial(attn_kernel, start, 4)
        near = [gain, state, first]
        return run(kernel, near, [], [vmem((16, E))], (acc, acc), 1 << 28)[0]

    local = attend(0, st_keep)
    local = local + attend(4, st_send)
    per_head = vmem((8, 8, E))
    p, s = run(rows_kernel, [gain], [local], [per_head, per_head], (), 1 << 28)
    far = [lax.ppermute(local, "head", [(i, (i + k) % 4) for i in range(4)]) for k in (1, 3, 2)]
    whole = local + far[0] + far[1] + far[2]
    scale = lax.rsqrt(whole[:8] / D + 1e-06)
    sc = jnp.concatenate([scale, scale**3 * whole[8:] / D], axis=0)

    back_first, back_last, gd = run(grad_kernel, [gain, sc, p, s], [], [parts, parts, per_head], (acc, acc), 1 << 29)
    back_sums = back_first + back_last
    dq = mixed = None

    def back(start, count):
        def during(sent):
            nonlocal dq, mixed
            state = st_send if start >= 4 else st_keep
            out = pltpu.VMEM((count, ROWS, E), BF16)
            dq, mixed, zeros = run(
                functools.partial(back_kernel, start, count),
                [gain, sc, state, first, gd], [sent], [hbm(shape, BF16, dq), hbm(shape, BF16, mixed), token],
                (acc, out, out, sems((2, count))), count << 29,
            )
            return zeros[:1]

        return during

    lt, other = scan(back_sums, mask, True, (back(0, 2), back(2, 2), back(4, 2), back(6, 2)))
    lt_keep = lt + keep_where(mask, LOWER, other)
    lt_send = swap(lt + keep_where(mask, UPPER, back_sums[:4]))
    gk = gv = None
    for start, later in ((0, lt_keep), (4, lt_send)):
        out = pltpu.VMEM((4, ROWS, E), BF16)
        gk, gv = run(
            functools.partial(last_kernel, start, 4), [later, back_last], [],
            [hbm(shape, BF16, gk), hbm(shape, BF16, gv)], (out, out, sems((2, 4))), 1 << 28,
        )
    return mixed, dq, gk, gv


def solution(mesh):
    rows = P(("seqin", "seqout"), "head")
    return jax.shard_map(
        shards,
        mesh=mesh,
        in_specs=(rows, rows, rows, P("head"), rows),
        out_specs=(rows, rows, rows, rows),
        check_vma=False,
    )
```

```python
import functools

import jax
import jax.numpy as jnp
from jax import lax
from jax.experimental import pallas as pl
from jax.experimental.pallas import tpu as pltpu
from jax.sharding import PartitionSpec as P

E = 128
D = 4096
ROWS = 1024
BLOCK = 512
HALF = 256
AUG = E + 8
F32 = jnp.float32
BF16 = jnp.bfloat16
VMEM_LIMIT = 16 * 1024 * 1024
UNROLL = 2
ORDER = (2, 1, 3)
USE = (0, 2, 1, 3)
ROW_ORDER = (1, 3, 2)


def phi(x):
    xf = x.astype(F32)
    return jnp.where(xf > 0, xf + 1.0, jnp.exp(xf)).astype(BF16)


def slope(x):
    xf = x.astype(F32)
    return jnp.where(xf > 0, 1.0, jnp.exp(xf))


def split(x):
    hi = x.astype(BF16)
    return hi, (x - hi.astype(F32)).astype(BF16)


def dot(a, b, ca=1, cb=0):
    return lax.dot_general(a, b, (((ca,), (cb,)), ((), ())), preferred_element_type=F32)


def iota(shape, dim):
    return lax.broadcasted_iota(jnp.int32, shape, dim)


def column(row):
    return jnp.transpose(jnp.broadcast_to(row, (E, E)))


def columns(at):
    core = lax.rem(lax.axis_index("seqout"), 2)
    return pl.ds(pl.multiple_of(lax.rem(4 * core + at, 8) * E, E), E)


def each(count, body):
    def step(j, carry):
        body(j)
        return carry

    lax.fori_loop(0, count, step, 0, unroll=3 if count == 3 else UNROLL)


def block_sums(fk, v):
    kv = dot(fk, v, 0, 0)
    z = jnp.sum(fk.astype(F32), axis=0, keepdims=True)
    return jnp.concatenate([kv, jnp.broadcast_to(z, (8, E))], axis=0)


def sums_kernel(
    keys_ref, values_ref, queries_ref, cotangent_ref, q_ref, k_ref, v_ref, ct_ref, fq_ref, fk_ref, nd_ref, gr_ref, wt_ref, g_ref, first_ref, last_ref, mask_ref, sems
):
    half = ROWS // 2
    near = pl.ds(pl.multiple_of(half * lax.rem(lax.axis_index("seqout"), 2), half), half)
    away = pl.ds(pl.multiple_of(half - half * lax.rem(lax.axis_index("seqout"), 2), half), half)
    top, bottom = pl.ds(0, BLOCK), pl.ds(BLOCK, BLOCK)
    copies = []
    for at in ((top, near), (top, away), (bottom, slice(None))):
        for src, dst in ((keys_ref, k_ref), (values_ref, v_ref)):
            copies.append(pltpu.make_async_copy(src.at[at], dst.at[at], sems.at[len(copies)]))
    for src, dst in ((queries_ref, q_ref), (cotangent_ref, ct_ref)):
        copies.append(pltpu.make_async_copy(src, dst, sems.at[len(copies)]))
    for copy in copies:
        copy.start()
    write_masks(mask_ref)
    for step in range(4):
        b = step // 2
        rows = pl.ds(b * BLOCK, BLOCK)
        if step < 3:
            copies[2 * step].wait()
            copies[2 * step + 1].wait()

        def group(i):
            done = []
            for j in (4 * (step % 2) + 2 * i, 4 * (step % 2) + 2 * i + 1):
                cols = columns(j)
                fk = phi(k_ref[rows, cols])
                done.append((j, cols, fk, block_sums(fk, v_ref[rows, cols])))
            for j, cols, fk, part in done:
                fk_ref[rows, cols] = fk
                (last_ref if b else first_ref)[j] = part

        each(2, group)
    for copy in copies[6:]:
        copy.wait()


def intra_kernel(start, count, sent_ref, q_ref, k_ref, v_ref, ct_ref, fq_ref, fk_ref, nd_ref, gr_ref, wt_ref, g_ref, token_ref):
    token_ref[...] = jnp.zeros_like(token_ref)
    tri = iota((HALF, HALF), 0) >= iota((HALF, HALF), 1)
    up = iota((HALF, HALF), 0) <= iota((HALF, HALF), 1)
    ones = jnp.ones((BLOCK, E), BF16)

    def one(j):
        cols = columns(start + j)
        done = []
        for b in range(2):
            rows = pl.ds(b * BLOCK, BLOCK)
            fq, fk = phi(q_ref[rows, cols]), fk_ref[rows, cols]
            done.append((rows, fq))
            wt_ref[start + j, b, pl.ds(0, HALF), :] = jnp.where(up, dot(fk[:HALF], fq[:HALF], 1, 1), 0.0).astype(BF16)
            wt_ref[start + j, b, pl.ds(HALF, HALF), :] = dot(fk[:HALF], fq[HALF:], 1, 1).astype(BF16)
            wt_ref[start + j, b, pl.ds(2 * HALF, HALF), :] = jnp.where(up, dot(fk[HALF:], fq[HALF:], 1, 1), 0.0).astype(BF16)
            va = jnp.concatenate([v_ref[rows, cols], ones], axis=1)
            w00 = jnp.where(tri, dot(fq[:HALF], fk[:HALF], 1, 1), 0.0).astype(BF16)
            w10 = dot(fq[HALF:], fk[:HALF], 1, 1).astype(BF16)
            w11 = jnp.where(tri, dot(fq[HALF:], fk[HALF:], 1, 1), 0.0).astype(BF16)
            nd_ref[start + j, pl.ds(b * BLOCK, HALF), :] = dot(w00, va[:HALF])
            nd_ref[start + j, pl.ds(b * BLOCK + HALF, HALF), :] = dot(jnp.concatenate([w10, w11], axis=1), va)
        for rows, fq in done:
            fq_ref[rows, cols] = fq

    each(count, one)


def attn_kernel(start, count, gain_ref, st_ref, first_ref, q_ref, k_ref, v_ref, ct_ref, fq_ref, fk_ref, nd_ref, gr_ref, wt_ref, g_ref, sums_ref, sq_acc, pr_acc):
    sq_acc[...] = jnp.zeros_like(sq_acc)
    pr_acc[...] = jnp.zeros_like(pr_acc)

    def pair(i):
        for b in range(2):
            rows = pl.ds(b * BLOCK, BLOCK)
            squares, products = [], []
            for j in (2 * i, 2 * i + 1):
                cols = columns(start + j)
                aug = st_ref[j] + first_ref[start + j] if b else st_ref[j]
                s_hi, s_lo = split(aug[:E])
                n_hi, n_lo = split(column(aug[E : E + 1]))
                rhs = jnp.concatenate([jnp.concatenate([s_hi, n_hi], axis=1), jnp.concatenate([s_lo, n_lo], axis=1)], axis=0)
                fq = fq_ref[rows, cols]
                nd = nd_ref[start + j, rows, :] + dot(jnp.concatenate([fq, fq], axis=1), rhs)
                inv = 1.0 / nd[:, E:]
                attn = nd[:, :E] * inv
                nd_ref[start + j, rows, :] = jnp.concatenate([attn, inv], axis=1)
                squares.append(attn * attn)
                products.append(ct_ref[rows, cols].astype(F32) * gain_ref[:, cols] * attn)
            sq_acc[rows, :] += squares[0] + squares[1]
            pr_acc[rows, :] += products[0] + products[1]

    each(count // 2, pair)
    for i in range(8):
        rows = pl.ds(i * E, E)
        sums_ref[pl.ds(i, 1), :] = jnp.sum(jnp.transpose(sq_acc[rows, :]), axis=0, keepdims=True)
        sums_ref[pl.ds(8 + i, 1), :] = jnp.sum(jnp.transpose(pr_acc[rows, :]), axis=0, keepdims=True)


def spread(sc_ref, scale_ref, coef_ref):
    for i in range(8):
        rows = pl.ds(i * E, E)
        scale_ref[rows, :] = column(sc_ref[pl.ds(i, 1), :])
        if coef_ref is not None:
            coef_ref[rows, :] = column(sc_ref[pl.ds(8 + i, 1), :])


def rows_kernel(gain_ref, sent_ref, q_ref, k_ref, v_ref, ct_ref, fq_ref, fk_ref, nd_ref, gr_ref, wt_ref, g_ref, p_ref, s_ref):
    ones = jnp.ones((8, 2 * E), BF16)

    def row_sums(x):
        hi, lo = split(x)
        return dot(ones, jnp.concatenate([hi, lo], axis=1), 1, 1)[0:1]

    def one(j):
        cols = columns(j)
        for b in range(2):
            rows = pl.ds(b * BLOCK, BLOCK)
            attn, inv = nd_ref[j, rows, :E], nd_ref[j, rows, E:]
            wi = ct_ref[rows, cols].astype(F32) * gain_ref[:, cols] * inv
            ai = attn * inv
            p, s = row_sums(wi * attn), row_sums(ai * attn)
            gr_ref[j, rows, :] = wi
            nd_ref[j, rows, E:] = ai
            for i in range(4):
                p_ref[j, pl.ds(4 * b + i, 1), :] = p[:, i * E : (i + 1) * E]
                s_ref[j, pl.ds(4 * b + i, 1), :] = s[:, i * E : (i + 1) * E]

    each(8, one)


def grad_kernel(
    gain_ref, sc_ref, p_ref, s_ref, q_ref, k_ref, v_ref, ct_ref, fq_ref, fk_ref, nd_ref, gr_ref, wt_ref, g_ref, first_ref, last_ref, gd_ref, scale_ref, coef_ref
):
    spread(sc_ref, scale_ref, coef_ref)

    def group(i):
        done = []
        for j in (2 * i, 2 * i + 1):
            cols = columns(j)
            gd = sc_ref[8:16, :] * s_ref[j] - sc_ref[0:8, :] * p_ref[j]
            hi = gd.astype(BF16).astype(F32)
            for b in range(2):
                rows = pl.ds(b * BLOCK, BLOCK)
                g = (scale_ref[rows, :] * gr_ref[j, rows, :] - coef_ref[rows, :] * nd_ref[j, rows, E:]).astype(BF16)
                pieces = [jnp.concatenate([x[4 * b + i : 4 * b + i + 1] for i in range(4)], axis=1) for x in (hi, gd - hi)]
                pieces.append(jnp.zeros((14, BLOCK), F32))
                fq = fq_ref[rows, cols]
                rden = dot(jnp.concatenate(pieces, axis=0).astype(BF16), fq)
                rden = jnp.broadcast_to(rden[0:1] + rden[1:2], (8, E))
                done.append((j, b, rows, g, jnp.concatenate([dot(fq, g, 0, 0), rden], axis=0)))
            gd_ref[j] = gd
        for j, b, rows, g, part in done:
            g_ref[rows, pl.ds(pl.multiple_of(j * E, E), E)] = g
            (last_ref if b else first_ref)[j] = part

    each(4, group)


def back_kernel(
    start, count, gain_ref, sc_ref, st_ref, first_ref, gd_ref, sent_ref, q_ref, k_ref, v_ref, ct_ref, fq_ref, fk_ref, nd_ref, gr_ref, wt_ref, g_ref,
    dq_ref, mixed_ref, token_ref, scale_ref, dq_buf, mixed_buf, sems,
):
    token_ref[...] = jnp.zeros_like(token_ref)
    spread(sc_ref, scale_ref, None)
    low = iota((HALF, HALF), 0) >= iota((HALF, HALF), 1)

    def copies(j):
        cols = columns(start + j)
        return [
            pltpu.make_async_copy(dq_buf.at[j], dq_ref.at[:, cols], sems.at[0, j]),
            pltpu.make_async_copy(mixed_buf.at[j], mixed_ref.at[:, cols], sems.at[1, j]),
        ]

    def one(j):
        cols = columns(start + j)
        for b in range(2):
            rows = pl.ds(b * BLOCK, BLOCK)
            v, fq, fk = v_ref[rows, cols], fq_ref[rows, cols], fk_ref[rows, cols]
            g = g_ref[rows, pl.ds(pl.multiple_of((start + j) * E, E), E)]
            gd = jnp.concatenate([column(gd_ref[start + j, pl.ds(4 * b + i, 1), :]) for i in range(4)], axis=0)
            add0, add1 = (jnp.concatenate([x, x], axis=1) for x in (gd[:HALF], gd[HALF:]))
            m00 = jnp.where(low, dot(g[:HALF], v[:HALF], 1, 1) + add0, 0.0).astype(BF16)
            m10 = (dot(g[HALF:], v[:HALF], 1, 1) + add1).astype(BF16)
            m11 = jnp.where(low, dot(g[HALF:], v[HALF:], 1, 1) + add1, 0.0).astype(BF16)
            w00, w10, w11 = (wt_ref[start + j, b, pl.ds(i * HALF, HALF), :] for i in range(3))
            aug = st_ref[start + j] + first_ref[start + j] if b else st_ref[start + j]
            s_hi, s_lo = split(aug[:E])
            rhs = jnp.concatenate([s_hi, s_lo], axis=1)
            dfq = dot(jnp.concatenate([g, g], axis=1), rhs, 1, 1) + gd * aug[E : E + 1]
            dfq = dfq + jnp.concatenate([dot(m00, fk[:HALF]), dot(jnp.concatenate([m10, m11], axis=1), fk)], axis=0)
            dq_buf[j, rows, :] = (dfq * slope(q_ref[rows, cols])).astype(BF16)
            mixed_buf[j, rows, :] = (nd_ref[start + j, rows, :E] * scale_ref[rows, :] * gain_ref[:, cols]).astype(BF16)
            nd_ref[start + j, pl.ds(b * BLOCK, HALF), :E] = dot(jnp.concatenate([m00, m10], axis=0), fq, 0, 0)
            nd_ref[start + j, pl.ds(b * BLOCK + HALF, HALF), :E] = dot(m11, fq[HALF:], 0, 0)
            nd_ref[start + j, pl.ds(b * BLOCK, HALF), E:] = dot(jnp.concatenate([w00, w10], axis=1), g)
            nd_ref[start + j, pl.ds(b * BLOCK + HALF, HALF), E:] = dot(w11, g[HALF:])
        for copy in copies(j):
            copy.start()

    each(count, one)
    for j in range(count):
        for copy in copies(j):
            copy.wait()


def last_kernel(start, count, lt_ref, last_ref, q_ref, k_ref, v_ref, ct_ref, fq_ref, fk_ref, nd_ref, gr_ref, wt_ref, g_ref, gk_ref, gv_ref, gk_buf, gv_buf, sems):

    def copies(j):
        cols = columns(start + j)
        return [
            pltpu.make_async_copy(gk_buf.at[j], gk_ref.at[:, cols], sems.at[0, j]),
            pltpu.make_async_copy(gv_buf.at[j], gv_ref.at[:, cols], sems.at[1, j]),
        ]

    def group(i):
        for j in (2 * i, 2 * i + 1):
            cols = columns(start + j)
            for b in range(2):
                rows = pl.ds(b * BLOCK, BLOCK)
                v, fk = v_ref[rows, cols], fk_ref[rows, cols]
                aug = lt_ref[j] if b else lt_ref[j] + last_ref[start + j]
                l_hi, l_lo = split(aug[:E])
                dfk = dot(jnp.concatenate([v, v], axis=1), jnp.concatenate([l_hi, l_lo], axis=1), 1, 1)
                dfk = dfk + nd_ref[start + j, rows, :E] + aug[E : E + 1]
                dv = dot(jnp.concatenate([fk, fk], axis=1), jnp.concatenate([l_hi, l_lo], axis=0))
                gk_buf[j, rows, :] = (dfk * slope(k_ref[rows, cols])).astype(BF16)
                gv_buf[j, rows, :] = (dv + nd_ref[start + j, rows, E:]).astype(BF16)
        for j in (2 * i, 2 * i + 1):
            for copy in copies(j):
                copy.start()

    for i in range(count // 2):
        group(i)
    for j in range(count):
        for copy in copies(j):
            copy.wait()


def vmem(shape, dtype=F32, into=None):
    return pltpu.VMEM(shape, dtype), into


def hbm(shape, dtype, into=None):
    return pltpu.HBM(shape, dtype), into


def call(kernel, near, far, outs, scratch=(), flops=0):
    arrays = [pltpu.with_memory_space_constraint(a, pltpu.VMEM) for a in near]
    arrays += far
    specs = [pl.BlockSpec(memory_space=pltpu.VMEM)] * len(near) + [pl.BlockSpec(memory_space=pl.ANY)] * len(far)
    first, shapes, out_specs, aliases = len(arrays), [], [], {}
    for i, (shape, into) in enumerate(outs):
        space = pl.ANY if shape.memory_space == pltpu.HBM else pltpu.VMEM
        shapes.append(shape)
        out_specs.append(pl.BlockSpec(memory_space=space))
        if into is not None:
            aliases[len(arrays)] = i
            arrays.append(pltpu.with_memory_space_constraint(into, shape.memory_space))
            specs.append(pl.BlockSpec(memory_space=space))

    def body(*refs):
        bank, nd, gr, wt, *own = refs[len(arrays) :]
        kernel(*refs[:first], *(bank.at[i] for i in range(6)), nd, gr, wt, bank.at[6], *own)

    return pl.pallas_call(
        body,
        out_shape=shapes,
        in_specs=specs,
        out_specs=out_specs,
        scratch_shapes=list(scratch),
        input_output_aliases=aliases,
        compiler_params=pltpu.CompilerParams(vmem_limit_bytes=VMEM_LIMIT),
        cost_estimate=pl.CostEstimate(flops=flops, bytes_accessed=1 << 20, transcendentals=0),
    )(*arrays)


CORE = [(i, i ^ 1) for i in range(8)]


def send_x(x, k):
    return lax.ppermute(x, "seqout", [(i, (i + 2 * k) % 8) for i in range(8)])


def send_y(x, k):
    return lax.ppermute(x, "seqin", [(i, (i + k) % 4) for i in range(4)])


def swap(x):
    return lax.ppermute(x, "seqout", CORE)


TO, SOURCE, BEFORE, AFTER, LOWER, UPPER, ROW_BEFORE, ROW_AFTER, MASKS = 0, 16, 32, 48, 64, 65, 66, 70, 80


def write_masks(mask_ref):
    place = lax.axis_index("seqout")
    x, core = lax.div(place, 2), lax.rem(place, 2)

    def put(at, true):
        mask_ref[pl.ds(at, 1), :] = jnp.full((1, E), jnp.where(true, 1.0, 0.0), F32)

    for k in range(4):
        to = lax.rem(x + k, 4)
        for i in range(4):
            source = lax.rem(x + 4 - i, 4)
            put(TO + 4 * k + i, to == i)
            put(SOURCE + 4 * k + i, lax.rem(x + 4 - k, 4) == i)
            put(BEFORE + 4 * k + i, source < to)
            put(AFTER + 4 * k + i, source > to)
    y = lax.axis_index("seqin")
    for k in range(4):
        put(ROW_BEFORE + k, y >= k)
        put(ROW_AFTER + k, y < 4 - k)
    put(LOWER, core == 0)
    put(UPPER, core == 1)


def keep_where(mask, at, x):
    return jnp.where(mask[at : at + 1] > 0, x, 0.0)


def add(parts):
    return functools.reduce(lambda a, b: a + b, parts)


def scan(sums, mask, reverse, during):
    other = swap(sums[4:])
    total = sums[:4] + other
    got = {k: add([keep_where(mask, TO + 4 * k + h, total[h]) for h in range(4)]) for k in (*ORDER, 0)}
    own = got[0]
    for k in ORDER:
        got[k] = send_x(got[k], k)
    row = add([got[k] for k in USE]) + during[0](own)
    rows = []
    for k in ROW_ORDER:
        came = send_y(row, -k if reverse else k)
        rows.append(keep_where(mask, (ROW_AFTER if reverse else ROW_BEFORE) + k, came))
    base = rows[0] + rows[1] + rows[2] + during[1](row)
    at = AFTER if reverse else BEFORE
    came = {k: base + add([keep_where(mask, at + 4 * k + m, got[m]) for m in USE]) for k in (*ORDER, 0)}
    for k in ORDER:
        came[k] = send_x(came[k], k)
    zeros = during[2](base)
    out = [add([keep_where(mask, SOURCE + 4 * k + h, came[k]) for k in USE]) + zeros for h in range(4)]
    return jnp.stack(out), other


def shards(queries, keys, values, gain, cotangent):
    gain = gain.reshape(1, ROWS)
    shape = (ROWS, ROWS)
    aug = vmem((4, AUG, E))
    token = vmem((8, E))
    acc = pltpu.VMEM((ROWS, E), F32)
    sems = pltpu.SemaphoreType.DMA
    kept = {}
    sizes = {"bank": ((7, ROWS, ROWS), BF16), "nd": ((8, ROWS, 2 * E), F32), "gr": ((8, ROWS, E), F32)}
    sizes |= {"wt": ((8, 2, 3 * HALF, HALF), BF16)}

    def run(kernel, near, far, outs, scratch=(), flops=0):
        held = [vmem(*size, kept.get(name)) for name, size in sizes.items()]
        got = call(kernel, near, [pltpu.with_memory_space_constraint(a, pltpu.HBM) if a.shape == shape else a for a in far], held + outs, scratch, flops)
        kept.update(zip(sizes, got))
        return got[len(sizes) :]

    parts = vmem((8, AUG, E))
    far = [keys, values, queries, cotangent]
    first, last, mask = run(sums_kernel, [], far, [parts, parts, vmem((MASKS, E))], [sems((8,))], 1 << 28)
    sums = first + last

    def intra(start, count):
        def during(sent):
            kernel = functools.partial(intra_kernel, start, count)
            (zeros,) = run(kernel, [], [sent], [token], (), count << 28)
            return zeros[:1]

        return during

    st, other = scan(sums, mask, False, (intra(0, 3), intra(3, 3), intra(6, 2)))
    st_keep = st + keep_where(mask, UPPER, other)
    st_send = swap(st + keep_where(mask, LOWER, sums[:4]))

    def attend(start, state):
        kernel = functools.partial(attn_kernel, start, 4)
        near = [gain, state, first]
        return run(kernel, near, [], [vmem((16, E))], (acc, acc), 1 << 28)[0]

    local = attend(0, st_keep)
    local = local + attend(4, st_send)
    per_head = vmem((8, 8, E))
    p, s = run(rows_kernel, [gain], [local], [per_head, per_head], (), 1 << 28)
    far = [lax.ppermute(local, "head", [(i, (i + k) % 4) for i in range(4)]) for k in (1, 3, 2)]
    whole = local + far[0] + far[1] + far[2]
    scale = lax.rsqrt(whole[:8] / D + 1e-06)
    sc = jnp.concatenate([scale, scale**3 * whole[8:] / D], axis=0)

    back_first, back_last, gd = run(grad_kernel, [gain, sc, p, s], [], [parts, parts, per_head], (acc, acc), 1 << 29)
    back_sums = back_first + back_last
    dq = mixed = None
    states = jnp.concatenate([st_keep, st_send])

    def back(start, count):
        def during(sent):
            nonlocal dq, mixed
            out = pltpu.VMEM((count, ROWS, E), BF16)
            dq, mixed, zeros = run(
                functools.partial(back_kernel, start, count),
                [gain, sc, states, first, gd], [sent], [hbm(shape, BF16, dq), hbm(shape, BF16, mixed), token],
                (acc, out, out, sems((2, count))), count << 29,
            )
            return zeros[:1]

        return during

    lt, other = scan(back_sums, mask, True, (back(0, 3), back(3, 3), back(6, 2)))
    lt_keep = lt + keep_where(mask, LOWER, other)
    lt_send = swap(lt + keep_where(mask, UPPER, back_sums[:4]))
    gk = gv = None
    for start, later in ((0, lt_keep), (4, lt_send)):
        out = pltpu.VMEM((4, ROWS, E), BF16)
        gk, gv = run(
            functools.partial(last_kernel, start, 4), [later, back_last], [],
            [hbm(shape, BF16, gk), hbm(shape, BF16, gv)], (out, out, sems((2, 4))), 1 << 28,
        )
    return mixed, dq, gk, gv


def solution(mesh):
    rows = P(("seqin", "seqout"), "head")
    return jax.shard_map(
        shards,
        mesh=mesh,
        in_specs=(rows, rows, rows, P("head"), rows),
        out_specs=(rows, rows, rows, rows),
        check_vma=False,
    )
```

```python
import functools

import jax
import jax.numpy as jnp
from jax import lax
from jax.experimental import pallas as pl
from jax.experimental.pallas import tpu as pltpu
from jax.sharding import PartitionSpec as P

E = 128
D = 4096
ROWS = 1024
BLOCK = 512
HALF = 256
AUG = E + 8
F32 = jnp.float32
BF16 = jnp.bfloat16
VMEM_LIMIT = 16 * 1024 * 1024
UNROLL = 4
ORDER = (2, 1, 3)
USE = (0, 2, 1, 3)
ROW_ORDER = (1, 3, 2)


def phi(x):
    xf = x.astype(F32)
    return jnp.where(xf > 0, xf + 1.0, jnp.exp(xf)).astype(BF16)


def slope(x):
    xf = x.astype(F32)
    return jnp.where(xf > 0, 1.0, jnp.exp(xf))


def split(x):
    hi = x.astype(BF16)
    return hi, (x - hi.astype(F32)).astype(BF16)


def dot(a, b, ca=1, cb=0):
    return lax.dot_general(a, b, (((ca,), (cb,)), ((), ())), preferred_element_type=F32)


def iota(shape, dim):
    return lax.broadcasted_iota(jnp.int32, shape, dim)


def column(row):
    return jnp.transpose(jnp.broadcast_to(row, (E, E)))


def columns(at):
    core = lax.rem(lax.axis_index("seqout"), 2)
    return pl.ds(pl.multiple_of(lax.rem(4 * core + at, 8) * E, E), E)


def each(count, body):
    def step(j, carry):
        body(j)
        return carry

    lax.fori_loop(0, count, step, 0, unroll=3 if count == 3 else min(count, UNROLL))


def block_sums(fk, v):
    kv = dot(fk, v, 0, 0)
    z = jnp.sum(fk.astype(F32), axis=0, keepdims=True)
    return jnp.concatenate([kv, jnp.broadcast_to(z, (8, E))], axis=0)


def sums_kernel(
    keys_ref, values_ref, queries_ref, cotangent_ref, q_ref, k_ref, v_ref, ct_ref, fq_ref, fk_ref, nd_ref, gr_ref, wt_ref, g_ref, first_ref, last_ref, mask_ref, sems
):
    half = ROWS // 2
    near = pl.ds(pl.multiple_of(half * lax.rem(lax.axis_index("seqout"), 2), half), half)
    away = pl.ds(pl.multiple_of(half - half * lax.rem(lax.axis_index("seqout"), 2), half), half)
    top, bottom = pl.ds(0, BLOCK), pl.ds(BLOCK, BLOCK)
    copies = []
    for at in ((top, near), (top, away), (bottom, slice(None))):
        for src, dst in ((keys_ref, k_ref), (values_ref, v_ref)):
            copies.append(pltpu.make_async_copy(src.at[at], dst.at[at], sems.at[len(copies)]))
    for src, dst in ((queries_ref, q_ref), (cotangent_ref, ct_ref)):
        copies.append(pltpu.make_async_copy(src, dst, sems.at[len(copies)]))
    for copy in copies:
        copy.start()
    write_masks(mask_ref)
    for step in range(4):
        b = step // 2
        rows = pl.ds(b * BLOCK, BLOCK)
        if step < 3:
            copies[2 * step].wait()
            copies[2 * step + 1].wait()

        def group(i):
            done = []
            for j in (4 * (step % 2) + 2 * i, 4 * (step % 2) + 2 * i + 1):
                cols = columns(j)
                fk = phi(k_ref[rows, cols])
                done.append((j, cols, fk, block_sums(fk, v_ref[rows, cols])))
            for j, cols, fk, part in done:
                fk_ref[rows, cols] = fk
                (last_ref if b else first_ref)[j] = part

        each(2, group)
    for copy in copies[6:]:
        copy.wait()


def intra_kernel(start, count, sent_ref, q_ref, k_ref, v_ref, ct_ref, fq_ref, fk_ref, nd_ref, gr_ref, wt_ref, g_ref, token_ref):
    token_ref[...] = jnp.zeros_like(token_ref)
    tri = iota((HALF, HALF), 0) >= iota((HALF, HALF), 1)
    up = iota((HALF, HALF), 0) <= iota((HALF, HALF), 1)
    ones = jnp.ones((BLOCK, E), BF16)

    def one(j):
        cols = columns(start + j)
        done = []
        for b in range(2):
            rows = pl.ds(b * BLOCK, BLOCK)
            fq, fk = phi(q_ref[rows, cols]), fk_ref[rows, cols]
            done.append((rows, fq))
            wt_ref[start + j, b, pl.ds(0, HALF), :] = jnp.where(up, dot(fk[:HALF], fq[:HALF], 1, 1), 0.0).astype(BF16)
            wt_ref[start + j, b, pl.ds(HALF, HALF), :] = dot(fk[:HALF], fq[HALF:], 1, 1).astype(BF16)
            wt_ref[start + j, b, pl.ds(2 * HALF, HALF), :] = jnp.where(up, dot(fk[HALF:], fq[HALF:], 1, 1), 0.0).astype(BF16)
            va = jnp.concatenate([v_ref[rows, cols], ones], axis=1)
            w00 = jnp.where(tri, dot(fq[:HALF], fk[:HALF], 1, 1), 0.0).astype(BF16)
            w10 = dot(fq[HALF:], fk[:HALF], 1, 1).astype(BF16)
            w11 = jnp.where(tri, dot(fq[HALF:], fk[HALF:], 1, 1), 0.0).astype(BF16)
            nd_ref[start + j, pl.ds(b * BLOCK, HALF), :] = dot(w00, va[:HALF])
            nd_ref[start + j, pl.ds(b * BLOCK + HALF, HALF), :] = dot(jnp.concatenate([w10, w11], axis=1), va)
        for rows, fq in done:
            fq_ref[rows, cols] = fq

    each(count, one)


def attn_kernel(start, count, gain_ref, st_ref, first_ref, q_ref, k_ref, v_ref, ct_ref, fq_ref, fk_ref, nd_ref, gr_ref, wt_ref, g_ref, sums_ref, sq_acc, pr_acc):
    sq_acc[...] = jnp.zeros_like(sq_acc)
    pr_acc[...] = jnp.zeros_like(pr_acc)

    def pair(i):
        for b in range(2):
            rows = pl.ds(b * BLOCK, BLOCK)
            squares, products = [], []
            for j in (2 * i, 2 * i + 1):
                cols = columns(start + j)
                aug = st_ref[j] + first_ref[start + j] if b else st_ref[j]
                s_hi, s_lo = split(aug[:E])
                n_hi, n_lo = split(column(aug[E : E + 1]))
                rhs = jnp.concatenate([jnp.concatenate([s_hi, n_hi], axis=1), jnp.concatenate([s_lo, n_lo], axis=1)], axis=0)
                fq = fq_ref[rows, cols]
                nd = nd_ref[start + j, rows, :] + dot(jnp.concatenate([fq, fq], axis=1), rhs)
                inv = 1.0 / nd[:, E:]
                attn = nd[:, :E] * inv
                nd_ref[start + j, rows, :] = jnp.concatenate([attn, inv], axis=1)
                squares.append(attn * attn)
                products.append(ct_ref[rows, cols].astype(F32) * gain_ref[:, cols] * attn)
            sq_acc[rows, :] += squares[0] + squares[1]
            pr_acc[rows, :] += products[0] + products[1]

    each(count // 2, pair)
    for i in range(8):
        rows = pl.ds(i * E, E)
        sums_ref[pl.ds(i, 1), :] = jnp.sum(jnp.transpose(sq_acc[rows, :]), axis=0, keepdims=True)
        sums_ref[pl.ds(8 + i, 1), :] = jnp.sum(jnp.transpose(pr_acc[rows, :]), axis=0, keepdims=True)


def spread(sc_ref, scale_ref, coef_ref):
    for i in range(8):
        rows = pl.ds(i * E, E)
        scale_ref[rows, :] = column(sc_ref[pl.ds(i, 1), :])
        if coef_ref is not None:
            coef_ref[rows, :] = column(sc_ref[pl.ds(8 + i, 1), :])


def rows_kernel(gain_ref, sent_ref, q_ref, k_ref, v_ref, ct_ref, fq_ref, fk_ref, nd_ref, gr_ref, wt_ref, g_ref, p_ref, s_ref):
    ones = jnp.ones((8, 2 * E), BF16)

    def row_sums(x):
        hi, lo = split(x)
        return dot(ones, jnp.concatenate([hi, lo], axis=1), 1, 1)[0:1]

    def one(j):
        cols = columns(j)
        for b in range(2):
            rows = pl.ds(b * BLOCK, BLOCK)
            attn, inv = nd_ref[j, rows, :E], nd_ref[j, rows, E:]
            wi = ct_ref[rows, cols].astype(F32) * gain_ref[:, cols] * inv
            ai = attn * inv
            p, s = row_sums(wi * attn), row_sums(ai * attn)
            gr_ref[j, rows, :] = wi
            nd_ref[j, rows, E:] = ai
            for i in range(4):
                p_ref[j, pl.ds(4 * b + i, 1), :] = p[:, i * E : (i + 1) * E]
                s_ref[j, pl.ds(4 * b + i, 1), :] = s[:, i * E : (i + 1) * E]

    each(8, one)


def grad_kernel(
    gain_ref, sc_ref, p_ref, s_ref, q_ref, k_ref, v_ref, ct_ref, fq_ref, fk_ref, nd_ref, gr_ref, wt_ref, g_ref, first_ref, last_ref, gd_ref, scale_ref, coef_ref
):
    spread(sc_ref, scale_ref, coef_ref)

    def group(i):
        done = []
        for j in (2 * i, 2 * i + 1):
            cols = columns(j)
            gd = sc_ref[8:16, :] * s_ref[j] - sc_ref[0:8, :] * p_ref[j]
            hi = gd.astype(BF16).astype(F32)
            for b in range(2):
                rows = pl.ds(b * BLOCK, BLOCK)
                g = (scale_ref[rows, :] * gr_ref[j, rows, :] - coef_ref[rows, :] * nd_ref[j, rows, E:]).astype(BF16)
                pieces = [jnp.concatenate([x[4 * b + i : 4 * b + i + 1] for i in range(4)], axis=1) for x in (hi, gd - hi)]
                pieces.append(jnp.zeros((14, BLOCK), F32))
                fq = fq_ref[rows, cols]
                rden = dot(jnp.concatenate(pieces, axis=0).astype(BF16), fq)
                rden = jnp.broadcast_to(rden[0:1] + rden[1:2], (8, E))
                done.append((j, b, rows, g, jnp.concatenate([dot(fq, g, 0, 0), rden], axis=0)))
            gd_ref[j] = gd
        for j, b, rows, g, part in done:
            g_ref[rows, pl.ds(pl.multiple_of(j * E, E), E)] = g
            (last_ref if b else first_ref)[j] = part

    each(4, group)


def back_kernel(
    start, count, gain_ref, sc_ref, st_ref, first_ref, gd_ref, sent_ref, q_ref, k_ref, v_ref, ct_ref, fq_ref, fk_ref, nd_ref, gr_ref, wt_ref, g_ref,
    dq_ref, mixed_ref, token_ref, scale_ref, dq_buf, mixed_buf, sems,
):
    token_ref[...] = jnp.zeros_like(token_ref)
    spread(sc_ref, scale_ref, None)
    low = iota((HALF, HALF), 0) >= iota((HALF, HALF), 1)

    def copies(j):
        cols = columns(start + j)
        return [
            pltpu.make_async_copy(dq_buf.at[j], dq_ref.at[:, cols], sems.at[0, j]),
            pltpu.make_async_copy(mixed_buf.at[j], mixed_ref.at[:, cols], sems.at[1, j]),
        ]

    def one(j):
        cols = columns(start + j)
        for b in range(2):
            rows = pl.ds(b * BLOCK, BLOCK)
            v, fq, fk = v_ref[rows, cols], fq_ref[rows, cols], fk_ref[rows, cols]
            g = g_ref[rows, pl.ds(pl.multiple_of((start + j) * E, E), E)]
            gd = jnp.concatenate([column(gd_ref[start + j, pl.ds(4 * b + i, 1), :]) for i in range(4)], axis=0)
            add0, add1 = (jnp.concatenate([x, x], axis=1) for x in (gd[:HALF], gd[HALF:]))
            m00 = jnp.where(low, dot(g[:HALF], v[:HALF], 1, 1) + add0, 0.0).astype(BF16)
            m10 = (dot(g[HALF:], v[:HALF], 1, 1) + add1).astype(BF16)
            m11 = jnp.where(low, dot(g[HALF:], v[HALF:], 1, 1) + add1, 0.0).astype(BF16)
            w00, w10, w11 = (wt_ref[start + j, b, pl.ds(i * HALF, HALF), :] for i in range(3))
            aug = st_ref[start + j] + first_ref[start + j] if b else st_ref[start + j]
            s_hi, s_lo = split(aug[:E])
            rhs = jnp.concatenate([s_hi, s_lo], axis=1)
            dfq = dot(jnp.concatenate([g, g], axis=1), rhs, 1, 1) + gd * aug[E : E + 1]
            dfq = dfq + jnp.concatenate([dot(m00, fk[:HALF]), dot(jnp.concatenate([m10, m11], axis=1), fk)], axis=0)
            dq_buf[j, rows, :] = (dfq * slope(q_ref[rows, cols])).astype(BF16)
            mixed_buf[j, rows, :] = (nd_ref[start + j, rows, :E] * scale_ref[rows, :] * gain_ref[:, cols]).astype(BF16)
            nd_ref[start + j, pl.ds(b * BLOCK, HALF), :E] = dot(jnp.concatenate([m00, m10], axis=0), fq, 0, 0)
            nd_ref[start + j, pl.ds(b * BLOCK + HALF, HALF), :E] = dot(m11, fq[HALF:], 0, 0)
            nd_ref[start + j, pl.ds(b * BLOCK, HALF), E:] = dot(jnp.concatenate([w00, w10], axis=1), g)
            nd_ref[start + j, pl.ds(b * BLOCK + HALF, HALF), E:] = dot(w11, g[HALF:])
        for copy in copies(j):
            copy.start()

    each(count, one)
    for j in range(count):
        for copy in copies(j):
            copy.wait()


def last_kernel(start, count, lt_ref, last_ref, q_ref, k_ref, v_ref, ct_ref, fq_ref, fk_ref, nd_ref, gr_ref, wt_ref, g_ref, gk_ref, gv_ref, gk_buf, gv_buf, sems):

    def copies(j):
        cols = columns(start + j)
        return [
            pltpu.make_async_copy(gk_buf.at[j], gk_ref.at[:, cols], sems.at[0, j]),
            pltpu.make_async_copy(gv_buf.at[j], gv_ref.at[:, cols], sems.at[1, j]),
        ]

    def group(i):
        for j in (2 * i, 2 * i + 1):
            cols = columns(start + j)
            for b in range(2):
                rows = pl.ds(b * BLOCK, BLOCK)
                v, fk = v_ref[rows, cols], fk_ref[rows, cols]
                aug = lt_ref[j] if b else lt_ref[j] + last_ref[start + j]
                l_hi, l_lo = split(aug[:E])
                dfk = dot(jnp.concatenate([v, v], axis=1), jnp.concatenate([l_hi, l_lo], axis=1), 1, 1)
                dfk = dfk + nd_ref[start + j, rows, :E] + aug[E : E + 1]
                dv = dot(jnp.concatenate([fk, fk], axis=1), jnp.concatenate([l_hi, l_lo], axis=0))
                gk_buf[j, rows, :] = (dfk * slope(k_ref[rows, cols])).astype(BF16)
                gv_buf[j, rows, :] = (dv + nd_ref[start + j, rows, E:]).astype(BF16)
        for j in (2 * i, 2 * i + 1):
            for copy in copies(j):
                copy.start()

    for i in range(count // 2):
        group(i)
    for j in range(count):
        for copy in copies(j):
            copy.wait()


def vmem(shape, dtype=F32, into=None):
    return pltpu.VMEM(shape, dtype), into


def hbm(shape, dtype, into=None):
    return pltpu.HBM(shape, dtype), into


def call(kernel, near, far, outs, scratch=(), flops=0):
    arrays = [pltpu.with_memory_space_constraint(a, pltpu.VMEM) for a in near]
    arrays += far
    specs = [pl.BlockSpec(memory_space=pltpu.VMEM)] * len(near) + [pl.BlockSpec(memory_space=pl.ANY)] * len(far)
    first, shapes, out_specs, aliases = len(arrays), [], [], {}
    for i, (shape, into) in enumerate(outs):
        space = pl.ANY if shape.memory_space == pltpu.HBM else pltpu.VMEM
        shapes.append(shape)
        out_specs.append(pl.BlockSpec(memory_space=space))
        if into is not None:
            aliases[len(arrays)] = i
            arrays.append(pltpu.with_memory_space_constraint(into, shape.memory_space))
            specs.append(pl.BlockSpec(memory_space=space))

    def body(*refs):
        bank, nd, gr, wt, *own = refs[len(arrays) :]
        kernel(*refs[:first], *(bank.at[i] for i in range(6)), nd, gr, wt, bank.at[6], *own)

    return pl.pallas_call(
        body,
        out_shape=shapes,
        in_specs=specs,
        out_specs=out_specs,
        scratch_shapes=list(scratch),
        input_output_aliases=aliases,
        compiler_params=pltpu.CompilerParams(vmem_limit_bytes=VMEM_LIMIT),
        cost_estimate=pl.CostEstimate(flops=flops, bytes_accessed=1 << 20, transcendentals=0),
    )(*arrays)


CORE = [(i, i ^ 1) for i in range(8)]


def send_x(x, k):
    return lax.ppermute(x, "seqout", [(i, (i + 2 * k) % 8) for i in range(8)])


def send_y(x, k):
    return lax.ppermute(x, "seqin", [(i, (i + k) % 4) for i in range(4)])


def swap(x):
    return lax.ppermute(x, "seqout", CORE)


TO, SOURCE, BEFORE, AFTER, LOWER, UPPER, ROW_BEFORE, ROW_AFTER, MASKS = 0, 16, 32, 48, 64, 65, 66, 70, 80


def write_masks(mask_ref):
    place = lax.axis_index("seqout")
    x, core = lax.div(place, 2), lax.rem(place, 2)

    def put(at, true):
        mask_ref[pl.ds(at, 1), :] = jnp.full((1, E), jnp.where(true, 1.0, 0.0), F32)

    for k in range(4):
        to = lax.rem(x + k, 4)
        for i in range(4):
            source = lax.rem(x + 4 - i, 4)
            put(TO + 4 * k + i, to == i)
            put(SOURCE + 4 * k + i, lax.rem(x + 4 - k, 4) == i)
            put(BEFORE + 4 * k + i, source < to)
            put(AFTER + 4 * k + i, source > to)
    y = lax.axis_index("seqin")
    for k in range(4):
        put(ROW_BEFORE + k, y >= k)
        put(ROW_AFTER + k, y < 4 - k)
    put(LOWER, core == 0)
    put(UPPER, core == 1)


def keep_where(mask, at, x):
    return jnp.where(mask[at : at + 1] > 0, x, 0.0)


def add(parts):
    return functools.reduce(lambda a, b: a + b, parts)


def scan(sums, mask, reverse, during):
    other = swap(sums[4:])
    total = sums[:4] + other + during[0](sums)
    got = {k: add([keep_where(mask, TO + 4 * k + h, total[h]) for h in range(4)]) for k in (*ORDER, 0)}
    own = got[0]
    for k in ORDER:
        got[k] = send_x(got[k], k)
    row = add([got[k] for k in USE]) + during[1](own)
    rows = []
    for k in ROW_ORDER:
        came = send_y(row, -k if reverse else k)
        rows.append(keep_where(mask, (ROW_AFTER if reverse else ROW_BEFORE) + k, came))
    base = rows[0] + rows[1] + rows[2] + during[2](row)
    at = AFTER if reverse else BEFORE
    came = {k: base + add([keep_where(mask, at + 4 * k + m, got[m]) for m in USE]) for k in (*ORDER, 0)}
    for k in ORDER:
        came[k] = send_x(came[k], k)
    zeros = during[3](base)
    out = [add([keep_where(mask, SOURCE + 4 * k + h, came[k]) for k in USE]) + zeros for h in range(4)]
    return jnp.stack(out), other


def shards(queries, keys, values, gain, cotangent):
    gain = gain.reshape(1, ROWS)
    shape = (ROWS, ROWS)
    aug = vmem((4, AUG, E))
    token = vmem((8, E))
    acc = pltpu.VMEM((ROWS, E), F32)
    sems = pltpu.SemaphoreType.DMA
    kept = {}
    sizes = {"bank": ((7, ROWS, ROWS), BF16), "nd": ((8, ROWS, 2 * E), F32), "gr": ((8, ROWS, E), F32)}
    sizes |= {"wt": ((8, 2, 3 * HALF, HALF), BF16)}

    def run(kernel, near, far, outs, scratch=(), flops=0):
        held = [vmem(*size, kept.get(name)) for name, size in sizes.items()]
        got = call(kernel, near, [pltpu.with_memory_space_constraint(a, pltpu.HBM) if a.shape == shape else a for a in far], held + outs, scratch, flops)
        kept.update(zip(sizes, got))
        return got[len(sizes) :]

    parts = vmem((8, AUG, E))
    far = [keys, values, queries, cotangent]
    first, last, mask = run(sums_kernel, [], far, [parts, parts, vmem((MASKS, E))], [sems((8,))], 1 << 28)
    sums = first + last

    def intra(start, count):
        def during(sent):
            kernel = functools.partial(intra_kernel, start, count)
            (zeros,) = run(kernel, [], [sent], [token], (), count << 28)
            return zeros[:1]

        return during

    st, other = scan(sums, mask, False, (intra(0, 2), intra(2, 2), intra(4, 2), intra(6, 2)))
    st_keep = st + keep_where(mask, UPPER, other)
    st_send = swap(st + keep_where(mask, LOWER, sums[:4]))

    def attend(start, state):
        kernel = functools.partial(attn_kernel, start, 4)
        near = [gain, state, first]
        return run(kernel, near, [], [vmem((16, E))], (acc, acc), 1 << 28)[0]

    local = attend(0, st_keep)
    local = local + attend(4, st_send)
    per_head = vmem((8, 8, E))
    p, s = run(rows_kernel, [gain], [local], [per_head, per_head], (), 1 << 28)
    far = [lax.ppermute(local, "head", [(i, (i + k) % 4) for i in range(4)]) for k in (1, 3, 2)]
    whole = local + far[0] + far[1] + far[2]
    scale = lax.rsqrt(whole[:8] / D + 1e-06)
    sc = jnp.concatenate([scale, scale**3 * whole[8:] / D], axis=0)

    back_first, back_last, gd = run(grad_kernel, [gain, sc, p, s], [], [parts, parts, per_head], (acc, acc), 1 << 29)
    back_sums = back_first + back_last
    dq = mixed = None
    states = jnp.concatenate([st_keep, st_send])

    def back(start, count):
        def during(sent):
            nonlocal dq, mixed
            out = pltpu.VMEM((count, ROWS, E), BF16)
            dq, mixed, zeros = run(
                functools.partial(back_kernel, start, count),
                [gain, sc, states, first, gd], [sent], [hbm(shape, BF16, dq), hbm(shape, BF16, mixed), token],
                (acc, out, out, sems((2, count))), count << 29,
            )
            return zeros[:1]

        return during

    lt, other = scan(back_sums, mask, True, (back(0, 1), back(1, 2), back(3, 3), back(6, 2)))
    lt_keep = lt + keep_where(mask, LOWER, other)
    lt_send = swap(lt + keep_where(mask, UPPER, back_sums[:4]))
    gk = gv = None
    for start, later in ((0, lt_keep), (4, lt_send)):
        out = pltpu.VMEM((4, ROWS, E), BF16)
        gk, gv = run(
            functools.partial(last_kernel, start, 4), [later, back_last], [],
            [hbm(shape, BF16, gk), hbm(shape, BF16, gv)], (out, out, sems((2, 4))), 1 << 28,
        )
    return mixed, dq, gk, gv


def solution(mesh):
    rows = P(("seqin", "seqout"), "head")
    return jax.shard_map(
        shards,
        mesh=mesh,
        in_specs=(rows, rows, rows, P("head"), rows),
        out_specs=(rows, rows, rows, rows),
        check_vma=False,
    )
```
